128 devices in a mesh: face: 4 (over x_hi, core), tile: 32 (over x_lo, z, y).
Axes of the slice: x: 4 (x_hi: 2, x_lo: 2; x = x_hi * 2 + x_lo), y: 4, z: 4, core: 2. Of those that a mesh axis runs over, the one named last changes fastest.
Arguments:
- atmos: bfloat16 [64, 768, 2048], P(None, 'tile', 'face'), may hold values from -6 to 6
- ocean: bfloat16 [64, 262144], P(None, ('face', 'tile')), may hold values from -6 to 6
- surface_heat_weight: float32 [64], replicated, may hold values from -4 to 4
- air_conv_first_weight: bfloat16 [3, 3, 64, 64], replicated, may hold values from -0.25 to 0.25
- air_conv_second_weight: bfloat16 [3, 3, 64, 64], replicated, may hold values from -0.25 to 0.25
- marine_conv_first_weight: bfloat16 [9, 64, 64], replicated, may hold values from -0.25 to 0.25
- marine_conv_second_weight: bfloat16 [9, 64, 64], replicated, may hold values from -0.25 to 0.25
- marine_coupling_slot: int32 [262144], P(('face', 'tile')), may hold values from 0 to 4095, as said below
- coupling_air_cells: int32 [128, 4096], P(('face', 'tile')), may hold values from 0 to 12287
- marine_neighbour_index: int32 [9, 262144], P(None, ('face', 'tile')), may hold values from 0 to 2559, as said below
Outputs:
- atmos_next: bfloat16 [64, 768, 2048], P(None, 'tile', 'face')
- ocean_next: bfloat16 [64, 262144], P(None, ('face', 'tile'))
The draws below stay inside these ranges and needn't reach their ends.
Inputs may be any that keep to these rules, and one draw needn't show every extreme that they name: `marine_coupling_slot`: within one ocean device's 2048 entries the values are distinct; value // 32 is the atmosphere device serving the cell, so no atmosphere device serves more than 32 cells of one ocean device, and on every ocean device some atmosphere device serves exactly 32. `marine_neighbour_index`: entry [k, g] lies within 256 of the cell's own position 256 + g % 2048; every device's entries reach both ends.
All inputs are finite; a program needn't handle non-finite values.
Results may differ from the reference program's by a relative error of at most 0.0064.
Values may be sent and summed in bfloat16 or wider, within the bound.
A program may use at most 128 MiB of HBM per device.

```python
import jax
import jax.numpy as jnp
from jax import lax

LEVEL_CHANNELS = 64
AR = 24
ACOL = 512
OCN = 2048
HALO = 256
K = 9
CAP = 32
GRID_ROWS = 768
GRID_COLUMNS = 2048
OCELLS = 262144
N_TILE = 32
DEVICES = 128


def draw_marine_coupling_slot(key, part):
    key = jax.random.fold_in(key, 11)
    device_count = OCELLS // OCN
    slot_space = 2 * OCN

    def one_block(block_key):
        first_key, second_key, third_key = jax.random.split(block_key, 3)
        order_scores = jax.random.permutation(first_key, slot_space).astype(jnp.int32)
        favoured = jax.random.randint(second_key, (), 0, device_count)
        slots = jnp.arange(slot_space, dtype=jnp.int32)
        scores = order_scores + jnp.where(slots // CAP == favoured, 0, slot_space)
        scores = jnp.where(slots == 0, -2, scores)
        scores = jnp.where(slots == slot_space - 1, -1, scores)
        chosen = jnp.argsort(scores, stable=True)[:OCN].astype(jnp.int32)
        shuffle = jax.random.permutation(third_key, OCN)
        return chosen[shuffle].astype(jnp.int32)
    block_keys = jax.random.split(key, device_count)
    return jax.vmap(one_block)(block_keys).reshape(-1).astype(jnp.int32)


def draw_marine_neighbour_index(key, part):
    key = jax.random.fold_in(key, 23)
    offsets = jax.random.randint(key, (K, OCELLS), -HALO, HALO + 1).astype(jnp.int32)
    within = (jnp.arange(OCELLS, dtype=jnp.int32) % OCN)[None, :]
    taps = jnp.arange(K, dtype=jnp.int32)[:, None]
    offsets = jnp.where((within == 0) & (taps == 0), -HALO, offsets)
    offsets = jnp.where((within == OCN - 1) & (taps == K - 1), HALO, offsets)
    return (HALO + within + offsets).astype(jnp.int32)


def plant(drawn, own_key, smallest, largest):
    longest = drawn.shape.index(max(drawn.shape))
    spots = []
    for shift in (0, 1):
        where = [jax.random.randint(jax.random.fold_in(own_key, axis), (), 0, length) for axis, length in enumerate(drawn.shape)]
        where[longest] = (where[longest] + shift) % drawn.shape[longest]
        spots.append(tuple(where))
    return drawn.at[spots[0]].set(smallest).at[spots[1]].set(largest)


def levels(rng, shape, cuts, smallest, top_value):
    factor_of = 1.0
    for dim, shards_of in cuts:
        heights = jax.random.uniform(jax.random.fold_in(jax.random.fold_in(rng, 6), dim), (shards_of,), jnp.float32, smallest / len(cuts), top_value / len(cuts))
        factor_of = factor_of * jnp.repeat(jnp.exp(heights), shape[dim] // shards_of).reshape((-1,) + (1,) * (len(shape) - 1 - dim))
    return factor_of


def noise(stream_key, dims, spread, reach, cuts=(), kind=jnp.bfloat16):
    loudness = levels(stream_key, dims, cuts, -0.22, 0.18) if cuts else 1.0
    drawn = jax.random.normal(stream_key, dims, jnp.float32) * spread * loudness
    return jnp.minimum(jnp.maximum(drawn, -reach), reach).astype(kind)


def setup_inputs(seed: int = 0) -> dict:
    splits = jax.random.split(jax.random.key(seed), 11)
    atmos = noise(splits[0], (LEVEL_CHANNELS, GRID_ROWS, GRID_COLUMNS), 1.0, 6.0, ((1, 32), (2, 4)))
    ocean = noise(splits[1], (LEVEL_CHANNELS, OCELLS), 1.0, 6.0, ((1, 128),))
    surface_heat_weight = noise(splits[2], (LEVEL_CHANNELS,), 1.0, 4.0, (), jnp.float32)
    air_conv_first_weight = noise(splits[3], (3, 3, LEVEL_CHANNELS, LEVEL_CHANNELS), (9 * LEVEL_CHANNELS) ** -0.5, 0.25)
    air_conv_second_weight = noise(splits[4], (3, 3, LEVEL_CHANNELS, LEVEL_CHANNELS), (9 * LEVEL_CHANNELS) ** -0.5, 0.25)
    marine_conv_first_weight = noise(splits[5], (K, LEVEL_CHANNELS, LEVEL_CHANNELS), (K * LEVEL_CHANNELS) ** -0.5, 0.25)
    marine_conv_second_weight = noise(splits[6], (K, LEVEL_CHANNELS, LEVEL_CHANNELS), (K * LEVEL_CHANNELS) ** -0.5, 0.25)
    marine_coupling_slot = draw_marine_coupling_slot(jax.random.fold_in(splits[10], 71), 0)
    coupling_air_cells = plant(jax.random.randint(splits[8], (DEVICES, DEVICES * CAP), 0, AR * ACOL), jax.random.fold_in(splits[8], 1), 0, (AR * ACOL) - 1).astype(jnp.int32)
    marine_neighbour_index = draw_marine_neighbour_index(jax.random.fold_in(splits[10], 71), 0)
    return {"atmos": atmos, "ocean": ocean, "surface_heat_weight": surface_heat_weight, "air_conv_first_weight": air_conv_first_weight, "air_conv_second_weight": air_conv_second_weight, "marine_conv_first_weight": marine_conv_first_weight, "marine_conv_second_weight": marine_conv_second_weight, "marine_coupling_slot": marine_coupling_slot, "coupling_air_cells": coupling_air_cells, "marine_neighbour_index": marine_neighbour_index}


def atmosphere_conv(values, weight):
    padded = jnp.pad(values, ((0, 0), (1, 1), (0, 0)))
    padded = jnp.concatenate([padded[:, :, -1:], padded, padded[:, :, :1]], axis=2)
    channels, row_total, column_total = values.shape
    summed = jnp.zeros((channels, row_total * column_total), jnp.float32)
    for row_tap in range(3):
        for col_tap in range(3):
            window = padded[:, row_tap:row_tap + row_total, col_tap:col_tap + column_total].reshape(channels, -1)
            summed = summed + jnp.dot(weight[row_tap, col_tap], window, preferred_element_type=jnp.float32)
    return summed.reshape(channels, row_total, column_total)


def ocean_layer(values, weight, neighbours):
    padded = jnp.pad(values, ((0, 0), (HALO, HALO)))
    device_count = OCELLS // OCN

    def one_device(device):
        window = lax.dynamic_slice_in_dim(padded, device * OCN, OCN + 2 * HALO, 1)
        taps_here = lax.dynamic_slice_in_dim(neighbours, device * OCN, OCN, 1)
        summed = jnp.zeros((values.shape[0], OCN), jnp.float32)
        for tap in range(K):
            summed = summed + jnp.dot(weight[tap], jnp.take(window, taps_here[tap], axis=1), preferred_element_type=jnp.float32)
        return summed

    blocks = lax.map(one_device, jnp.arange(device_count, dtype=jnp.int32))
    return jnp.transpose(blocks, (1, 0, 2)).reshape(values.shape[0], OCELLS)


def reference(atmos, ocean, surface_heat_weight, air_conv_first_weight, air_conv_second_weight, marine_conv_first_weight, marine_conv_second_weight, marine_coupling_slot, coupling_air_cells, marine_neighbour_index):
    device = jnp.arange(OCELLS, dtype=jnp.int32) // OCN
    source = marine_coupling_slot // CAP
    position = marine_coupling_slot % CAP
    local_cell = coupling_air_cells[source, device * CAP + position]
    face_index = source // N_TILE
    tile_index = source % N_TILE
    row_index = tile_index * AR + local_cell // ACOL
    col_index = face_index * ACOL + local_cell % ACOL
    flat_cell = row_index * GRID_COLUMNS + col_index
    overall_sums = jnp.zeros((GRID_ROWS * GRID_COLUMNS,), jnp.float32).at[flat_cell].add(ocean[0].astype(jnp.float32))
    running_counts = jnp.zeros((GRID_ROWS * GRID_COLUMNS,), jnp.float32).at[flat_cell].add(jnp.ones((OCELLS,), jnp.float32))
    surface_heat_field = (overall_sums / jnp.maximum(running_counts, 1.0)).reshape(GRID_ROWS, GRID_COLUMNS)
    begin_offset = (atmos.astype(jnp.float32) + surface_heat_weight[:, None, None] * surface_heat_field[None]).astype(jnp.bfloat16)
    hidden = jax.nn.gelu(atmosphere_conv(begin_offset, air_conv_first_weight)).astype(jnp.bfloat16)
    atmos_next = (begin_offset.astype(jnp.float32) + atmosphere_conv(hidden, air_conv_second_weight)).astype(jnp.bfloat16)
    forcing = jnp.take(atmos_next.reshape(atmos.shape[0], -1), flat_cell, axis=1)
    ocean_start = (ocean.astype(jnp.float32) + forcing.astype(jnp.float32)).astype(jnp.bfloat16)
    ocean_hidden = jax.nn.gelu(ocean_layer(ocean_start, marine_conv_first_weight, marine_neighbour_index)).astype(jnp.bfloat16)
    ocean_next = (ocean_start.astype(jnp.float32) + ocean_layer(ocean_hidden, marine_conv_second_weight, marine_neighbour_index)).astype(jnp.bfloat16)
    return atmos_next, ocean_next
```

```python
import jax
import jax.numpy as jnp
from jax import lax
from jax.experimental import pallas as pl
from jax.experimental.pallas import tpu as pltpu
from jax.sharding import PartitionSpec as P

MESH = pl.DeviceIdType.MESH
BF = jnp.bfloat16
F32 = jnp.float32
I32 = jnp.int32
FACES = 4
TILES = 32
DEVICES = 128
CAP = 32
CH = 64
AR = 24
AC = 512
OCN = 2048
SLOTS = 4096
HALO = 256
EXT = OCN + 2 * HALO
RING = AC + 128
TAPS = 9


def iota(shape, dim):
    return lax.broadcasted_iota(I32, shape, dim)


def dot(a, b):
    return jnp.dot(a, b, preferred_element_type=F32)


def dot_nt(a, b):
    return lax.dot_general(a, b, (((1,), (1,)), ((), ())), preferred_element_type=F32)


def onehot(mask):
    return jnp.where(mask, 1.0, 0.0).astype(BF)


def where_of(number):
    return (lax.div(number, TILES), lax.rem(number, TILES))


def kernel(
    air, ocean, heat, w1, w2, m1, m2, slot, cells, taps,
    air_out, ocean_out,
    vsend, vrecv, cols, rcols, rrows, sst, sx, hx, acc, weights, picked_cols, table, onecol,
    gsend, grecv, arrived, oneslot, mweights, window, hwindow, picked,
    a_send, a_recv, r_send, r_recv, s_send, s_recv, g_send, g_recv, o_send, o_recv,
):
    face = lax.axis_index("face")
    tile = lax.axis_index("tile")
    me = face * TILES + tile

    barrier = pltpu.get_barrier_semaphore()

    def greet(step, carry):
        other = lax.rem(me + step, DEVICES)
        pl.semaphore_signal(barrier, inc=1, device_id=where_of(other), device_id_type=MESH)
        return carry

    lax.fori_loop(1, DEVICES, greet, 0)

    slots = slot[...]
    heat_row = ocean[0:16, :].astype(F32)[0:1]
    source = onehot(iota((DEVICES, OCN), 0) == slots // CAP)
    place = iota((DEVICES, OCN), 0)
    position = slots % CAP
    values = jnp.where(place == position, heat_row, 0.0)
    values = jnp.where(place == position + CAP, 1.0, values).astype(BF)
    vsend[:, 0, :] = dot_nt(source, values)

    lane = iota((CH, 128), 1)

    def pack_row(row, carry):
        left, right = carry
        first = jnp.where(lane < 2, air[row, :, 0:128].astype(F32), 0.0)
        last = jnp.where(lane >= 126, air[row, :, AC - 128 : AC].astype(F32), 0.0)
        left = left + pltpu.roll(first, 2 * row, 1)
        right = right + pltpu.roll(last, 2 * row + 2, 1)
        return left, right

    zero = jnp.zeros((CH, 128), F32)
    left, right = lax.fori_loop(0, AR, pack_row, (zero, zero))
    cols[0] = left.astype(BF)
    cols[1] = right.astype(BF)

    pl.semaphore_wait(barrier, DEVICES - 1)

    def send_values(step, carry):
        other = lax.rem(me + step, DEVICES)
        pltpu.make_async_remote_copy(
            src_ref=vsend.at[other], dst_ref=vrecv.at[me], send_sem=a_send, recv_sem=a_recv,
            device_id=where_of(other), device_id_type=MESH,
        ).start()
        return carry

    lax.fori_loop(1, DEVICES, send_values, 0)
    vrecv[me] = vsend[me]

    up = lax.rem(tile + TILES - 1, TILES)
    down = lax.rem(tile + 1, TILES)
    west = lax.rem(face + FACES - 1, FACES)
    east = lax.rem(face + 1, FACES)
    around = (
        (face, up), (face, down), (west, tile), (east, tile),
        (west, up), (west, down), (east, up), (east, down),
    )

    def rim(number, src, dst, send, recv):
        return pltpu.make_async_remote_copy(
            src_ref=src, dst_ref=dst, send_sem=send.at[number], recv_sem=recv.at[number],
            device_id=around[number], device_id_type=MESH,
        )

    air_rims = [
        rim(0, air.at[0:2], rrows.at[1], r_send, r_recv),
        rim(1, air.at[AR - 2 : AR], rrows.at[0], r_send, r_recv),
        rim(2, cols.at[0], rcols.at[1], r_send, r_recv),
        rim(3, cols.at[1], rcols.at[0], r_send, r_recv),
        rim(4, cols.at[0], rcols.at[5], r_send, r_recv),
        rim(5, cols.at[0], rcols.at[3], r_send, r_recv),
        rim(6, cols.at[1], rcols.at[4], r_send, r_recv),
        rim(7, cols.at[1], rcols.at[2], r_send, r_recv),
    ]
    for copy in air_rims:
        copy.start()

    def make_columns(step, carry):
        base = pl.multiple_of(step * 256, 256)
        column = cells[0:1, pl.ds(base, 256)] % AC
        onecol[:, pl.ds(base, 256)] = onehot(iota((AC, 256), 0) == column)
        return carry

    lax.fori_loop(0, SLOTS // 256, make_columns, 0)
    for number, weight in enumerate((w1, w2)):
        for row_tap in range(3):
            for col_tap in range(3):
                weights[number, row_tap * CH : (row_tap + 1) * CH, col_tap * CH : (col_tap + 1) * CH] = weight[
                    row_tap, col_tap
                ]
    for number, weight in enumerate((m1, m2)):
        for tap in range(TAPS):
            mweights[number, :, tap * CH : (tap + 1) * CH] = weight[tap]
    channel_weight = jnp.sum(
        jnp.where(iota((CH, CH), 0) == iota((CH, CH), 1), heat[...], 0.0), axis=1, keepdims=True
    )

    for copy in air_rims:
        copy.wait()

    def ring_block(row, left, right):
        from_right = pltpu.roll(right, lax.rem(128 - 2 * row, 128), 1)
        from_left = pltpu.roll(left, lax.rem(254 - 2 * row, 128), 1)
        return jnp.where(lane < 64, from_right, from_left).astype(BF)

    def extend(row, carry):
        sx[row + 2, :, 0:AC] = air[row]
        sx[row + 2, :, AC:RING] = ring_block(row, rcols[0].astype(F32), rcols[1].astype(F32))
        return carry

    lax.fori_loop(0, AR, extend, 0)
    for row in range(2):
        sx[row, :, 0:AC] = rrows[0, row]
        sx[row, :, AC:RING] = ring_block(jnp.int32(AR - 2 + row), rcols[2].astype(F32), rcols[3].astype(F32))
        sx[AR + 2 + row, :, 0:AC] = rrows[1, row]
        sx[AR + 2 + row, :, AC:RING] = ring_block(jnp.int32(row), rcols[4].astype(F32), rcols[5].astype(F32))

    pltpu.make_async_copy(vrecv.at[pl.ds(0, DEVICES - 1)], vrecv.at[pl.ds(0, DEVICES - 1)], a_recv).wait()
    got = vrecv[:, 0, :].astype(BF)
    square = (DEVICES, 128)
    mine = iota(square, 0) % 4 == iota(square, 1) // CAP
    group = onehot(iota((CAP, DEVICES), 0) == iota((CAP, DEVICES), 1) // 4)
    for kind in range(2):
        expand = onehot(iota(square, 0) - CAP * kind == iota(square, 1) % CAP)
        spread = jnp.where(mine, dot(got, expand), 0.0).astype(BF)
        table[kind] = dot(group, spread)

    def make_rows(step, carry):
        base = pl.multiple_of(step * 128, 128)
        row = cells[0:1, pl.ds(base, 128)] // AC
        hit = iota((CAP, 128), 0) == row
        for kind in range(2):
            picked_cols[CAP * kind : CAP * (kind + 1), pl.ds(base, 128)] = jnp.where(
                hit, table[kind, pl.ds(step, 1), :], 0.0
            ).astype(BF)
        return carry

    lax.fori_loop(0, SLOTS // 128, make_rows, 0)
    sums = dot_nt(picked_cols[...], onecol[...])
    sst[8 : 8 + AR, 128 : 128 + AC] = sums[0:AR] / jnp.maximum(sums[CAP : CAP + AR], 1.0)

    top, low, far = 128, 640, 768
    sst_rims = [
        rim(0, sst.at[8:16, top:low], sst.at[32:40, top:low], s_send, s_recv),
        rim(1, sst.at[24:32, top:low], sst.at[0:8, top:low], s_send, s_recv),
        rim(2, sst.at[8:32, 128:256], sst.at[8:32, low:far], s_send, s_recv),
        rim(3, sst.at[8:32, 512:640], sst.at[8:32, 0:128], s_send, s_recv),
        rim(4, sst.at[8:16, 128:256], sst.at[32:40, low:far], s_send, s_recv),
        rim(5, sst.at[24:32, 128:256], sst.at[0:8, low:far], s_send, s_recv),
        rim(6, sst.at[8:16, 512:640], sst.at[32:40, 0:128], s_send, s_recv),
        rim(7, sst.at[24:32, 512:640], sst.at[0:8, 0:128], s_send, s_recv),
    ]
    for copy in sst_rims:
        copy.start()
    for copy in sst_rims:
        copy.wait()

    low_lane = iota((1, 128), 1) < 64

    def begin(row, carry):
        line = sst[pl.ds(row + 6, 1), :]
        ring = jnp.concatenate(
            [line[:, 128 : 128 + AC], jnp.where(low_lane, line[:, 640:768], line[:, 0:128])], axis=1
        )
        state = sx[row].astype(F32) + channel_weight * ring
        inside = jnp.logical_and(jnp.logical_or(row >= 2, tile > 0), jnp.logical_or(row < AR + 2, tile < TILES - 1))
        sx[row] = jnp.where(inside, state, 0.0).astype(BF)
        return carry

    lax.fori_loop(0, AR + 4, begin, 0)

    def three(x, width):
        wide = x.astype(F32)
        before = pltpu.roll(wide, 1, 1).astype(BF)[:, 0:width]
        after = pltpu.roll(wide, RING - 1, 1).astype(BF)[:, 0:width]
        return jnp.concatenate([before, x[:, 0:width], after], axis=0)

    def first_conv(row, carry):
        part = dot(weights[0], three(sx[row], RING))
        total = acc[0] + part[2 * CH : 3 * CH]
        acc[0] = acc[1] + part[CH : 2 * CH]
        acc[1] = part[0:CH]
        middle = row - 2
        inside = jnp.logical_and(jnp.logical_or(middle >= 1, tile > 0), jnp.logical_or(middle < AR + 1, tile < TILES - 1))
        hidden = jnp.where(inside, jax.nn.gelu(total, approximate=True), 0.0)
        hx[jnp.maximum(middle, 0)] = hidden.astype(BF)
        return carry

    lax.fori_loop(0, AR + 4, first_conv, 0)

    def second_conv(row, carry):
        part = dot(weights[1], three(hx[row], AC))
        total = acc[0, :, 0:AC] + part[2 * CH : 3 * CH]
        acc[0, :, 0:AC] = acc[1, :, 0:AC] + part[CH : 2 * CH]
        acc[1, :, 0:AC] = part[0:CH]
        middle = jnp.maximum(row - 2, 0)
        air_out[middle] = (sx[middle + 2, :, 0:AC].astype(F32) + total).astype(BF)
        return carry

    lax.fori_loop(0, AR + 2, second_conv, 0)

    def coupling(step, carry):
        block = lax.rem(lax.div(me, 8) + step, DEVICES // 8)
        base = pl.multiple_of(block * 256, 256)
        row = cells[0:1, pl.ds(base, 256)] // AC
        select = onecol[:, pl.ds(base, 256)]
        state = jnp.zeros((CH, 256), F32)
        for part in range(AR // 4):
            rows = air_out[part * 4 : part * 4 + 4].reshape(4 * CH, AC)
            found = dot(rows, select)
            for inner in range(4):
                state = jnp.where(row == part * 4 + inner, found[inner * CH : (inner + 1) * CH], state)
        flat = jnp.transpose(state).reshape(8, CAP, CH)
        pair = jnp.concatenate([flat[:, 0:16], flat[:, 16:32]], axis=2)
        gsend[pl.ds(pl.multiple_of(block * 8, 8), 8)] = pair.astype(BF)
        for inner in range(8):
            other = block * 8 + inner

            @pl.when(other != me)
            def _():
                pltpu.make_async_remote_copy(
                    src_ref=gsend.at[other], dst_ref=grecv.at[me], send_sem=g_send, recv_sem=g_recv,
                    device_id=where_of(other), device_id_type=MESH,
                ).start()

        return carry

    lax.fori_loop(0, DEVICES // 8, coupling, 0)
    grecv[me] = gsend[me]

    def make_slots(step, carry):
        base = pl.multiple_of(step * 256, 256)
        mark = slot[0:1, pl.ds(base, 256)]
        row = mark // CAP * 16 + mark % 16

        def fill(part, inner_carry):
            first = pl.multiple_of(part * 256, 256)
            oneslot[pl.ds(first, 256), pl.ds(base, 256)] = onehot(iota((256, 256), 0) + first == row)
            return inner_carry

        return lax.fori_loop(0, OCN // 256, fill, carry)

    lax.fori_loop(0, OCN // 256, make_slots, 0)
    pltpu.make_async_copy(grecv.at[pl.ds(0, DEVICES - 1)], grecv.at[pl.ds(0, DEVICES - 1)], g_recv).wait()

    def turn(step, carry):
        eight = grecv[pl.ds(pl.multiple_of(step * 8, 8), 8)].reshape(128, 128)
        arrived[:, pl.ds(pl.multiple_of(step * 128, 128), 128)] = jnp.transpose(eight.astype(F32)).astype(BF)
        return carry

    lax.fori_loop(0, DEVICES // 8, turn, 0)

    def force(step, carry):
        base = pl.multiple_of(step * 256, 256)
        late = (slot[0:1, pl.ds(base, 256)] // 16) % 2 == 1
        found = dot(arrived[...], oneslot[:, pl.ds(base, 256)])
        forcing = jnp.where(late, found[CH : 2 * CH], found[0:CH])
        begun = ocean[:, pl.ds(base, 256)].astype(F32) + forcing
        window[:, pl.ds(base + HALO, 256)] = begun.astype(BF).astype(F32)
        return carry

    lax.fori_loop(0, OCN // 256, force, 0)

    before = where_of(lax.rem(me + DEVICES - 1, DEVICES))
    after = where_of(lax.rem(me + 1, DEVICES))

    def ocean_rims(buffer, first):
        return [
            pltpu.make_async_remote_copy(
                src_ref=buffer.at[:, HALO : 2 * HALO], dst_ref=buffer.at[:, EXT - HALO : EXT],
                send_sem=o_send.at[first], recv_sem=o_recv.at[first], device_id=before, device_id_type=MESH,
            ),
            pltpu.make_async_remote_copy(
                src_ref=buffer.at[:, OCN : OCN + HALO], dst_ref=buffer.at[:, 0:HALO],
                send_sem=o_send.at[first + 1], recv_sem=o_recv.at[first + 1], device_id=after, device_id_type=MESH,
            ),
        ]

    def mix(buffer, number, block):
        for half in range(2):
            base = pl.multiple_of(block * 256 + half * 128, 128)
            parts = [
                [
                    buffer[group * 8 : (group + 1) * 8, pl.ds(pl.multiple_of(base + part * 128, 128), 128)]
                    for part in range(5)
                ]
                for group in range(CH // 8)
            ]
            for tap in range(TAPS):
                index = jnp.broadcast_to(taps[tap : tap + 1, pl.ds(base, 128)] - base, (8, 128))
                inner = index % 128
                part_of = index // 128
                groups = []
                for group in range(CH // 8):
                    found = jnp.take_along_axis(parts[group][0], inner, axis=1)
                    for part in range(1, 5):
                        found = jnp.where(
                            part_of == part, jnp.take_along_axis(parts[group][part], inner, axis=1), found
                        )
                    groups.append(found)
                picked[tap * CH : (tap + 1) * CH, half * 128 : (half + 1) * 128] = jnp.concatenate(
                    groups, axis=0
                ).astype(BF)
        return dot(mweights[number], picked[...])

    def hidden_block(block):
        total = mix(window, 0, block)
        base = pl.multiple_of(block * 256, 256)
        hwindow[:, pl.ds(base + HALO, 256)] = jax.nn.gelu(total, approximate=True).astype(BF).astype(F32)

    def last_block(block):
        total = mix(hwindow, 1, block)
        base = pl.multiple_of(block * 256, 256)
        ocean_out[:, pl.ds(base, 256)] = (window[:, pl.ds(base + HALO, 256)] + total).astype(BF)

    def close_ends(buffer):
        @pl.when(me == 0)
        def _():
            buffer[:, 0:HALO] = jnp.zeros((CH, HALO), F32)

        @pl.when(me == DEVICES - 1)
        def _():
            buffer[:, EXT - HALO : EXT] = jnp.zeros((CH, HALO), F32)

    def layer(buffer, first, do_block):
        copies = ocean_rims(buffer, first)
        for copy in copies:
            copy.start()

        def middle(block, carry):
            do_block(block)
            return carry

        lax.fori_loop(1, 7, middle, 0)
        for copy in copies:
            copy.wait()
        close_ends(buffer)

        def ends(step, carry):
            do_block(step * 7)
            return carry

        lax.fori_loop(0, 2, ends, 0)

    layer(window, 0, hidden_block)
    layer(hwindow, 2, last_block)

    pltpu.make_async_copy(vsend.at[pl.ds(0, DEVICES - 1)], vsend.at[pl.ds(0, DEVICES - 1)], a_send).wait()
    pltpu.make_async_copy(gsend.at[pl.ds(0, DEVICES - 1)], gsend.at[pl.ds(0, DEVICES - 1)], g_send).wait()


def shards(atmos, ocean, heat, w1, w2, m1, m2, slot, cells, taps):
    vmem = pl.BlockSpec(memory_space=pltpu.VMEM)
    dma = pltpu.SemaphoreType.DMA
    air = jnp.transpose(atmos, (1, 0, 2))
    air_next, ocean_next = pl.pallas_call(
        kernel,
        out_shape=(
            jax.ShapeDtypeStruct((AR, CH, AC), BF),
            jax.ShapeDtypeStruct((CH, OCN), BF),
        ),
        in_specs=[vmem] * 10,
        out_specs=(vmem, vmem),
        scratch_shapes=[
            pltpu.VMEM((DEVICES, 1, 128), F32),
            pltpu.VMEM((DEVICES, 1, 128), F32),
            pltpu.VMEM((2, CH, 128), BF),
            pltpu.VMEM((6, CH, 128), BF),
            pltpu.VMEM((2, 2, CH, AC), BF),
            pltpu.VMEM((40, 768), F32),
            pltpu.VMEM((AR + 4, CH, RING), BF),
            pltpu.VMEM((AR + 2, CH, RING), BF),
            pltpu.VMEM((2, CH, RING), F32),
            pltpu.VMEM((2, 3 * CH, 3 * CH), BF),
            pltpu.VMEM((2 * CAP, SLOTS), BF),
            pltpu.VMEM((2, CAP, 128), F32),
            pltpu.VMEM((AC, SLOTS), BF),
            pltpu.VMEM((DEVICES, 16, 128), BF),
            pltpu.VMEM((DEVICES, 16, 128), BF),
            pltpu.VMEM((128, OCN), BF),
            pltpu.VMEM((OCN, OCN), BF),
            pltpu.VMEM((2, CH, TAPS * CH), BF),
            pltpu.VMEM((CH, EXT), F32),
            pltpu.VMEM((CH, EXT), F32),
            pltpu.VMEM((TAPS * CH, 256), BF),
            dma, dma, dma((8,)), dma((8,)), dma((8,)), dma((8,)), dma, dma, dma((4,)), dma((4,)),
        ],
        compiler_params=pltpu.CompilerParams(
            collective_id=0, has_side_effects=True, vmem_limit_bytes=56 << 20
        ),
        name="level",
    )(air, ocean, heat.reshape(1, CH), w1, w2, m1, m2, slot.reshape(1, OCN), cells, taps)
    return jnp.transpose(air_next, (1, 0, 2)), ocean_next


def solution(mesh):
    placed = (
        P(None, "tile", "face"),
        P(None, ("face", "tile")),
        P(),
        P(),
        P(),
        P(),
        P(),
        P(("face", "tile")),
        P(("face", "tile"), None),
        P(None, ("face", "tile")),
    )
    return jax.shard_map(
        shards,
        mesh=mesh,
        in_specs=placed,
        out_specs=(P(None, "tile", "face"), P(None, ("face", "tile"))),
        check_vma=False,
    )
```

```python
import jax
import jax.numpy as jnp
from jax import lax
from jax.experimental import pallas as pl
from jax.experimental.pallas import tpu as pltpu
from jax.sharding import PartitionSpec as P

MESH = pl.DeviceIdType.MESH
BF = jnp.bfloat16
F32 = jnp.float32
I32 = jnp.int32
FACES = 4
TILES = 32
DEVICES = 128
CAP = 32
CH = 64
AR = 24
AC = 512
OCN = 2048
SLOTS = 4096
HALO = 256
EXT = OCN + 2 * HALO
RING = AC + 128
TAPS = 9


def iota(shape, dim):
    return lax.broadcasted_iota(I32, shape, dim)


def dot(a, b):
    return jnp.dot(a, b, preferred_element_type=F32)


def dot_nt(a, b):
    return lax.dot_general(a, b, (((1,), (1,)), ((), ())), preferred_element_type=F32)


def onehot(mask):
    return jnp.where(mask, 1.0, 0.0).astype(BF)


def where_of(number):
    return (lax.div(number, TILES), lax.rem(number, TILES))


def kernel(
    air, ocean, heat, w1, w2, m1, m2, slot, cells, taps,
    air_out, ocean_out,
    air_in, w1_in, w2_in, m1_in, m2_in, taps_in, air_done, after,
    vsend, vrecv, cols, rcols, sst, sx, hx, acc, weights, picked_cols, table, onecol,
    gsend, grecv, arrived, oneslot, onetap, mweights, window, hwindow,
    local, a_send, a_recv, r_send, r_recv, s_send, s_recv, g_send, g_recv, o_send, o_recv,
):
    face = lax.axis_index("face")
    tile = lax.axis_index("tile")
    me = face * TILES + tile

    barrier = pltpu.get_barrier_semaphore()

    def greet(step, carry):
        other = lax.rem(me + step, DEVICES)
        pl.semaphore_signal(barrier, inc=1, device_id=where_of(other), device_id_type=MESH)
        return carry

    lax.fori_loop(1, DEVICES, greet, 0)

    loads = [
        pltpu.make_async_copy(src, dst, local.at[number])
        for number, (src, dst) in enumerate(
            ((air, air_in), (w1, w1_in), (w2, w2_in), (m1, m1_in), (m2, m2_in), (taps, taps_in))
        )
    ]
    for copy in loads:
        copy.start()

    slots = slot[...]
    heat_row = ocean[0:16, :].astype(F32)[0:1]
    source = onehot(iota((DEVICES, OCN), 0) == slots // CAP)
    place = iota((DEVICES, OCN), 0)
    position = slots % CAP
    values = jnp.where(place == position, heat_row, 0.0)
    values = jnp.where(place == position + CAP, 1.0, values).astype(BF)
    vsend[:, 0, :] = dot_nt(source, values)

    pl.semaphore_wait(barrier, DEVICES - 1)

    def send_values(step, carry):
        other = lax.rem(me + step, DEVICES)
        pltpu.make_async_remote_copy(
            src_ref=vsend.at[other], dst_ref=vrecv.at[me], send_sem=a_send, recv_sem=a_recv,
            device_id=where_of(other), device_id_type=MESH,
        ).start()
        return carry

    lax.fori_loop(1, DEVICES, send_values, 0)
    vrecv[me] = vsend[me]

    for copy in loads:
        copy.wait()
    sx[2 : AR + 2, :, 0:AC] = pltpu.einshape("crw->rcw", air_in[...])

    lane = iota((CH, 128), 1)

    def pack_row(row, carry):
        left, right = carry
        first = jnp.where(lane < 2, sx[row + 2, :, 0:128].astype(F32), 0.0)
        last = jnp.where(lane >= 126, sx[row + 2, :, AC - 128 : AC].astype(F32), 0.0)
        left = left + pltpu.roll(first, 2 * row, 1)
        right = right + pltpu.roll(last, 2 * row + 2, 1)
        return left, right

    zero = jnp.zeros((CH, 128), F32)
    left, right = lax.fori_loop(0, AR, pack_row, (zero, zero), unroll=6)
    cols[0] = left.astype(BF)
    cols[1] = right.astype(BF)

    up = lax.rem(tile + TILES - 1, TILES)
    down = lax.rem(tile + 1, TILES)
    west = lax.rem(face + FACES - 1, FACES)
    east = lax.rem(face + 1, FACES)
    around = (
        (face, up), (face, down), (west, tile), (east, tile),
        (west, up), (west, down), (east, up), (east, down),
    )

    def rim(number, src, dst, send, recv):
        return pltpu.make_async_remote_copy(
            src_ref=src, dst_ref=dst, send_sem=send.at[number], recv_sem=recv.at[number],
            device_id=around[number], device_id_type=MESH,
        )

    air_rims = [
        rim(0, sx.at[2:4, :, 0:AC], sx.at[AR + 2 : AR + 4, :, 0:AC], r_send, r_recv),
        rim(1, sx.at[AR : AR + 2, :, 0:AC], sx.at[0:2, :, 0:AC], r_send, r_recv),
        rim(2, cols.at[0], rcols.at[1], r_send, r_recv),
        rim(3, cols.at[1], rcols.at[0], r_send, r_recv),
        rim(4, cols.at[0], rcols.at[5], r_send, r_recv),
        rim(5, cols.at[0], rcols.at[3], r_send, r_recv),
        rim(6, cols.at[1], rcols.at[4], r_send, r_recv),
        rim(7, cols.at[1], rcols.at[2], r_send, r_recv),
    ]
    for copy in air_rims:
        copy.start()

    def make_columns(step, carry):
        base = pl.multiple_of(step * 256, 256)
        column = cells[0:1, pl.ds(base, 256)] % AC
        onecol[:, pl.ds(base, 256)] = onehot(iota((AC, 256), 0) == column)
        return carry

    lax.fori_loop(0, SLOTS // 256, make_columns, 0, unroll=2)
    for number, weight in enumerate((w1_in, w2_in)):
        for row_tap in range(3):
            for col_tap in range(3):
                weights[number, row_tap * CH : (row_tap + 1) * CH, col_tap * CH : (col_tap + 1) * CH] = weight[
                    row_tap, col_tap
                ]
    for number, weight in enumerate((m1_in, m2_in)):
        for tap in range(TAPS):
            mweights[number, :, tap * CH : (tap + 1) * CH] = weight[tap]
    channel_weight = jnp.sum(
        jnp.where(iota((CH, CH), 0) == iota((CH, CH), 1), heat[...], 0.0), axis=1, keepdims=True
    )

    for copy in air_rims:
        copy.wait()

    def ring_block(row, left, right):
        from_right = pltpu.roll(right, lax.rem(128 - 2 * row, 128), 1)
        from_left = pltpu.roll(left, lax.rem(254 - 2 * row, 128), 1)
        return jnp.where(lane < 64, from_right, from_left).astype(BF)

    def extend(row, carry):
        sx[row + 2, :, AC:RING] = ring_block(row, rcols[0].astype(F32), rcols[1].astype(F32))
        return carry

    lax.fori_loop(0, AR, extend, 0, unroll=6)
    for row in range(2):
        sx[row, :, AC:RING] = ring_block(jnp.int32(AR - 2 + row), rcols[2].astype(F32), rcols[3].astype(F32))
        sx[AR + 2 + row, :, AC:RING] = ring_block(jnp.int32(row), rcols[4].astype(F32), rcols[5].astype(F32))

    pltpu.make_async_copy(vrecv.at[pl.ds(0, DEVICES - 1)], vrecv.at[pl.ds(0, DEVICES - 1)], a_recv).wait()
    got = vrecv[:, 0, :].astype(BF)
    square = (DEVICES, 128)
    mine = iota(square, 0) % 4 == iota(square, 1) // CAP
    group = onehot(iota((CAP, DEVICES), 0) == iota((CAP, DEVICES), 1) // 4)
    for kind in range(2):
        expand = onehot(iota(square, 0) - CAP * kind == iota(square, 1) % CAP)
        spread = jnp.where(mine, dot(got, expand), 0.0).astype(BF)
        table[kind] = dot(group, spread)

    def make_rows(step, carry):
        base = pl.multiple_of(step * 128, 128)
        row = cells[0:1, pl.ds(base, 128)] // AC
        hit = iota((CAP, 128), 0) == row
        for kind in range(2):
            picked_cols[CAP * kind : CAP * (kind + 1), pl.ds(base, 128)] = jnp.where(
                hit, table[kind, pl.ds(step, 1), :], 0.0
            ).astype(BF)
        return carry

    lax.fori_loop(0, SLOTS // 128, make_rows, 0, unroll=8)
    sums = dot_nt(picked_cols[...], onecol[...])
    sst[8 : 8 + AR, 128 : 128 + AC] = sums[0:AR] / jnp.maximum(sums[CAP : CAP + AR], 1.0)

    top, low, far = 128, 640, 768
    sst_rims = [
        rim(0, sst.at[8:16, top:low], sst.at[32:40, top:low], s_send, s_recv),
        rim(1, sst.at[24:32, top:low], sst.at[0:8, top:low], s_send, s_recv),
        rim(2, sst.at[8:32, 128:256], sst.at[8:32, low:far], s_send, s_recv),
        rim(3, sst.at[8:32, 512:640], sst.at[8:32, 0:128], s_send, s_recv),
        rim(4, sst.at[8:16, 128:256], sst.at[32:40, low:far], s_send, s_recv),
        rim(5, sst.at[24:32, 128:256], sst.at[0:8, low:far], s_send, s_recv),
        rim(6, sst.at[8:16, 512:640], sst.at[32:40, 0:128], s_send, s_recv),
        rim(7, sst.at[24:32, 512:640], sst.at[0:8, 0:128], s_send, s_recv),
    ]
    for copy in sst_rims:
        copy.start()
    for copy in sst_rims:
        copy.wait()

    low_lane = iota((1, 128), 1) < 64

    def begin(row, carry):
        line = sst[pl.ds(row + 6, 1), :]
        ring = jnp.concatenate(
            [line[:, 128 : 128 + AC], jnp.where(low_lane, line[:, 640:768], line[:, 0:128])], axis=1
        )
        state = sx[row].astype(F32) + channel_weight * ring
        inside = jnp.logical_and(jnp.logical_or(row >= 2, tile > 0), jnp.logical_or(row < AR + 2, tile < TILES - 1))
        sx[row] = jnp.where(inside, state, 0.0).astype(BF)
        return carry

    lax.fori_loop(0, AR + 4, begin, 0, unroll=7)

    def three(x, width):
        west_of = pltpu.roll(x, 1, 1)[:, 0:width]
        east_of = pltpu.roll(x, RING - 1, 1)[:, 0:width]
        return jnp.concatenate([west_of, x[:, 0:width], east_of], axis=0)

    def first_conv(row, carry):
        part = dot(weights[0], three(sx[row], RING))
        total = acc[0] + part[2 * CH : 3 * CH]
        acc[0] = acc[1] + part[CH : 2 * CH]
        acc[1] = part[0:CH]
        middle = row - 2
        inside = jnp.logical_and(jnp.logical_or(middle >= 1, tile > 0), jnp.logical_or(middle < AR + 1, tile < TILES - 1))
        hidden = jnp.where(inside, jax.nn.gelu(total, approximate=True), 0.0)
        hx[jnp.maximum(middle, 0)] = hidden.astype(BF)
        return carry

    lax.fori_loop(0, AR + 4, first_conv, 0, unroll=AR + 4)

    def second_conv(row, carry):
        part = dot(weights[1], three(hx[row], AC))
        total = acc[0, :, 0:AC] + part[2 * CH : 3 * CH]
        acc[0, :, 0:AC] = acc[1, :, 0:AC] + part[CH : 2 * CH]
        acc[1, :, 0:AC] = part[0:CH]
        middle = jnp.maximum(row - 2, 0)
        after[middle] = (sx[middle + 2, :, 0:AC].astype(F32) + total).astype(BF)
        return carry

    lax.fori_loop(0, AR + 2, second_conv, 0, unroll=AR + 2)

    first_block = lax.div(me, 8)

    def block_of(step):
        return lax.rem(first_block + step, DEVICES // 8)

    def find(block):
        base = pl.multiple_of(block * 256, 256)
        row = cells[0:1, pl.ds(base, 256)] // AC
        select = onecol[:, pl.ds(base, 256)]
        state = jnp.zeros((CH, 256), F32)
        for part in range(AR // 4):
            rows = after[part * 4 : part * 4 + 4].reshape(4 * CH, AC)
            found = dot(rows, select)
            for inner in range(4):
                state = jnp.where(row == part * 4 + inner, found[inner * CH : (inner + 1) * CH], state)
        return state

    def ship(state, block, others):
        flat = jnp.transpose(state).reshape(8, CAP, CH)
        pair = jnp.concatenate([flat[:, 0:16], flat[:, 16:32]], axis=2)
        gsend[pl.ds(pl.multiple_of(block * 8, 8), 8)] = pair.astype(BF)
        for inner in others:
            other = block * 8 + inner
            pltpu.make_async_remote_copy(
                src_ref=gsend.at[other], dst_ref=grecv.at[me], send_sem=g_send, recv_sem=g_recv,
                device_id=where_of(other), device_id_type=MESH,
            ).start()

    def coupling(step, state):
        found = find(block_of(step))
        ship(state, block_of(step - 1), range(8))
        return found

    state = lax.fori_loop(2, DEVICES // 8 + 1, coupling, find(block_of(1)), unroll=3)
    ship(state, first_block, [lax.rem(me + step, 8) for step in range(1, 8)])
    grecv[me] = gsend[me]

    air_done[...] = pltpu.einshape("rcw->crw", after[...])
    store = pltpu.make_async_copy(air_done, air_out, local.at[0])
    store.start()

    def make_slots(step, carry):
        base = pl.multiple_of(step * 256, 256)
        mark = slot[0:1, pl.ds(base, 256)]
        row = mark // CAP * 16 + mark % 16

        def fill(part, inner_carry):
            first = pl.multiple_of(part * 256, 256)
            oneslot[pl.ds(first, 256), pl.ds(base, 256)] = onehot(iota((256, 256), 0) + first == row)
            return inner_carry

        return lax.fori_loop(0, OCN // 256, fill, carry)

    lax.fori_loop(0, OCN // 256, make_slots, 0)

    def make_taps(step, carry):
        base = pl.multiple_of(step * 256, 256)
        for tap in range(TAPS):
            inner = (taps_in[tap : tap + 1, pl.ds(base, 256)] - base) % 256
            onetap[tap, :, pl.ds(base, 256)] = onehot(iota((256, 256), 0) == inner)
        return carry

    lax.fori_loop(0, OCN // 256, make_taps, 0)
    pltpu.make_async_copy(grecv.at[pl.ds(0, DEVICES - 1)], grecv.at[pl.ds(0, DEVICES - 1)], g_recv).wait()

    def turn(step, carry):
        eight = grecv[pl.ds(pl.multiple_of(step * 8, 8), 8)].reshape(128, 128)
        arrived[:, pl.ds(pl.multiple_of(step * 128, 128), 128)] = jnp.transpose(eight.astype(F32)).astype(BF)
        return carry

    lax.fori_loop(0, DEVICES // 8, turn, 0, unroll=8)

    def force(step, carry):
        base = pl.multiple_of(step * 256, 256)
        late = (slot[0:1, pl.ds(base, 256)] // 16) % 2 == 1
        found = dot(arrived[...], oneslot[:, pl.ds(base, 256)])
        forcing = jnp.where(late, found[CH : 2 * CH], found[0:CH])
        begun = ocean[:, pl.ds(base, 256)].astype(F32) + forcing
        window[:, pl.ds(base + HALO, 256)] = begun.astype(BF)
        return carry

    lax.fori_loop(0, OCN // 256, force, 0, unroll=4)

    previous = where_of(lax.rem(me + DEVICES - 1, DEVICES))
    following = where_of(lax.rem(me + 1, DEVICES))

    def ocean_rims(buffer, first):
        return [
            pltpu.make_async_remote_copy(
                src_ref=buffer.at[:, HALO : 2 * HALO], dst_ref=buffer.at[:, EXT - HALO : EXT],
                send_sem=o_send.at[first], recv_sem=o_recv.at[first], device_id=previous, device_id_type=MESH,
            ),
            pltpu.make_async_remote_copy(
                src_ref=buffer.at[:, OCN : OCN + HALO], dst_ref=buffer.at[:, 0:HALO],
                send_sem=o_send.at[first + 1], recv_sem=o_recv.at[first + 1], device_id=following, device_id_type=MESH,
            ),
        ]

    def mix(buffer, number, block):
        base = pl.multiple_of(block * 256, 256)
        segments = jnp.concatenate(
            [buffer[:, pl.ds(pl.multiple_of(base + 256 * part, 256), 256)] for part in range(3)], axis=0
        )
        groups = []
        for tap in range(TAPS):
            part_of = (taps_in[tap : tap + 1, pl.ds(base, 256)] - base) // 256
            found = dot(segments, onetap[tap, :, pl.ds(base, 256)])
            chosen = jnp.where(
                part_of == 0, found[0:CH], jnp.where(part_of == 1, found[CH : 2 * CH], found[2 * CH : 3 * CH])
            )
            groups.append(chosen.astype(BF))
        return dot(mweights[number], jnp.concatenate(groups, axis=0))

    def hidden_block(block):
        total = mix(window, 0, block)
        base = pl.multiple_of(block * 256, 256)
        hwindow[:, pl.ds(base + HALO, 256)] = jax.nn.gelu(total, approximate=True).astype(BF)

    def last_block(block):
        total = mix(hwindow, 1, block)
        base = pl.multiple_of(block * 256, 256)
        ocean_out[:, pl.ds(base, 256)] = (window[:, pl.ds(base + HALO, 256)].astype(F32) + total).astype(BF)

    def close_ends(buffer):
        @pl.when(me == 0)
        def _():
            buffer[:, 0:HALO] = jnp.zeros((CH, HALO), BF)

        @pl.when(me == DEVICES - 1)
        def _():
            buffer[:, EXT - HALO : EXT] = jnp.zeros((CH, HALO), BF)

    def layer(buffer, first, do_block):
        copies = ocean_rims(buffer, first)
        for copy in copies:
            copy.start()

        def middle(block, carry):
            do_block(block)
            return carry

        lax.fori_loop(1, 7, middle, 0, unroll=6)
        for copy in copies:
            copy.wait()
        close_ends(buffer)

        def ends(step, carry):
            do_block(step * 7)
            return carry

        lax.fori_loop(0, 2, ends, 0, unroll=2)

    layer(window, 0, hidden_block)
    layer(hwindow, 2, last_block)
    store.wait()

    pltpu.make_async_copy(vsend.at[pl.ds(0, DEVICES - 1)], vsend.at[pl.ds(0, DEVICES - 1)], a_send).wait()
    pltpu.make_async_copy(gsend.at[pl.ds(0, DEVICES - 1)], gsend.at[pl.ds(0, DEVICES - 1)], g_send).wait()


def hand_over(air, ocean, air_out, ocean_out, air_held, ocean_held, come, go):
    pieces = [(ocean, ocean_held, ocean_out)]
    for part in range(4):
        rows = pl.ds(part * 16, 16)
        pieces.append((air.at[rows], air_held.at[rows], air_out.at[rows]))
    inward = [pltpu.make_async_copy(src, held, come.at[i]) for i, (src, held, _) in enumerate(pieces)]
    outward = [pltpu.make_async_copy(held, dst, go.at[i]) for i, (_, held, dst) in enumerate(pieces)]
    for copy in inward:
        copy.start()
    for first, second in zip(inward, outward):
        first.wait()
        second.start()
    for copy in outward:
        copy.wait()


def shards(atmos, ocean, heat, w1, w2, m1, m2, slot, cells, taps):
    vmem = pl.BlockSpec(memory_space=pltpu.VMEM)
    dma = pltpu.SemaphoreType.DMA
    anywhere = pl.BlockSpec(memory_space=pl.ANY)
    results = pl.pallas_call(
        kernel,
        out_shape=(
            jax.ShapeDtypeStruct((CH, AR, AC), BF),
            jax.ShapeDtypeStruct((CH, OCN), BF),
        ),
        in_specs=[anywhere, vmem, vmem] + [anywhere] * 4 + [vmem, vmem, anywhere],
        out_specs=(anywhere, vmem),
        scratch_shapes=[
            pltpu.VMEM((CH, AR, AC), BF),
            pltpu.VMEM((3, 3, CH, CH), BF),
            pltpu.VMEM((3, 3, CH, CH), BF),
            pltpu.VMEM((TAPS, CH, CH), BF),
            pltpu.VMEM((TAPS, CH, CH), BF),
            pltpu.VMEM((TAPS, OCN), I32),
            pltpu.VMEM((CH, AR, AC), BF),
            pltpu.VMEM((AR, CH, AC), BF),
            pltpu.VMEM((DEVICES, 1, 128), F32),
            pltpu.VMEM((DEVICES, 1, 128), F32),
            pltpu.VMEM((2, CH, 128), BF),
            pltpu.VMEM((6, CH, 128), BF),
            pltpu.VMEM((40, 768), F32),
            pltpu.VMEM((AR + 4, CH, RING), BF),
            pltpu.VMEM((AR + 2, CH, RING), BF),
            pltpu.VMEM((2, CH, RING), F32),
            pltpu.VMEM((2, 3 * CH, 3 * CH), BF),
            pltpu.VMEM((2 * CAP, SLOTS), BF),
            pltpu.VMEM((2, CAP, 128), F32),
            pltpu.VMEM((AC, SLOTS), BF),
            pltpu.VMEM((DEVICES, 16, 128), BF),
            pltpu.VMEM((DEVICES, 16, 128), BF),
            pltpu.VMEM((128, OCN), BF),
            pltpu.VMEM((OCN, OCN), BF),
            pltpu.VMEM((TAPS, 256, OCN), BF),
            pltpu.VMEM((2, CH, TAPS * CH), BF),
            pltpu.VMEM((CH, EXT), BF),
            pltpu.VMEM((CH, EXT), BF),
            dma((6,)), dma, dma, dma((8,)), dma((8,)), dma((8,)), dma((8,)), dma, dma, dma((4,)), dma((4,)),
        ],
        compiler_params=pltpu.CompilerParams(
            collective_id=0, has_side_effects=True, vmem_limit_bytes=56 << 20
        ),
        name="level",
    )(atmos, ocean, heat.reshape(1, CH), w1, w2, m1, m2, slot.reshape(1, OCN), cells, taps)
    return pl.pallas_call(
        hand_over,
        out_shape=(
            jax.ShapeDtypeStruct((CH, AR, AC), BF),
            jax.ShapeDtypeStruct((CH, OCN), BF),
        ),
        in_specs=[anywhere, anywhere],
        out_specs=(anywhere, anywhere),
        scratch_shapes=[pltpu.VMEM((CH, AR, AC), BF), pltpu.VMEM((CH, OCN), BF), dma((5,)), dma((5,))],
        name="hand_over",
    )(*results)


def solution(mesh):
    placed = (
        P(None, "tile", "face"),
        P(None, ("face", "tile")),
        P(),
        P(),
        P(),
        P(),
        P(),
        P(("face", "tile")),
        P(("face", "tile"), None),
        P(None, ("face", "tile")),
    )
    return jax.shard_map(
        shards,
        mesh=mesh,
        in_specs=placed,
        out_specs=(P(None, "tile", "face"), P(None, ("face", "tile"))),
        check_vma=False,
    )
```

```python
import jax
import jax.numpy as jnp
from jax import lax
from jax.experimental import pallas as pl
from jax.experimental.pallas import tpu as pltpu
from jax.sharding import PartitionSpec as P

MESH = pl.DeviceIdType.MESH
BF = jnp.bfloat16
F32 = jnp.float32
I32 = jnp.int32
FACES = 4
TILES = 32
DEVICES = 128
CAP = 32
CH = 64
AR = 24
AC = 512
OCN = 2048
SLOTS = 4096
HALO = 256
EXT = OCN + 2 * HALO
RING = AC + 128
TAPS = 9


def iota(shape, dim):
    return lax.broadcasted_iota(I32, shape, dim)


def dot(a, b):
    return jnp.dot(a, b, preferred_element_type=F32)


def dot_nt(a, b):
    return lax.dot_general(a, b, (((1,), (1,)), ((), ())), preferred_element_type=F32)


def onehot(mask):
    return jnp.where(mask, 1.0, 0.0).astype(BF)


def where_of(number):
    return (lax.div(number, TILES), lax.rem(number, TILES))


def kernel(
    air, ocean, heat, w1, w2, m1, m2, slot, cells, taps,
    air_out, ocean_out,
    air_in, w1_in, w2_in, m1_in, m2_in, taps_in, air_done, after,
    vsend, vfirst, vturned, vrecv, cols, rcols, sst, sx, hx, acc, weights, picked_cols, onecol,
    gsend, grecv, arrived, oneslot, onetap, mweights, window, hwindow,
    local, a_send, a_recv, b_send, b_recv, r_send, r_recv, s_send, s_recv, g_send, g_recv, o_send, o_recv,
):
    face = lax.axis_index("face")
    tile = lax.axis_index("tile")
    me = face * TILES + tile

    outer = face * 2 + lax.div(tile, 16)
    inner_place = lax.rem(tile, 16)
    up = lax.rem(tile + TILES - 1, TILES)
    down = lax.rem(tile + 1, TILES)
    west = lax.rem(face + FACES - 1, FACES)
    east = lax.rem(face + 1, FACES)
    around = (
        (face, up), (face, down), (west, tile), (east, tile),
        (west, up), (west, down), (east, up), (east, down),
    )

    def outer_peer(number):
        return (lax.div(number, 2), lax.rem(number, 2) * 16 + inner_place)

    def inner_peer(number):
        return (face, lax.div(tile, 16) * 16 + number)

    barrier = pltpu.get_barrier_semaphore()
    greeted = [outer_peer(lax.rem(outer + step, 8)) for step in range(1, 8)]
    greeted += [inner_peer(lax.rem(inner_place + step, 16)) for step in range(1, 16)]
    greeted += list(around)
    for other in greeted:
        pl.semaphore_signal(barrier, inc=1, device_id=other, device_id_type=MESH)

    loads = [
        pltpu.make_async_copy(src, dst, local.at[number])
        for number, (src, dst) in enumerate(
            ((air, air_in), (w1, w1_in), (w2, w2_in), (m1, m1_in), (m2, m2_in), (taps, taps_in))
        )
    ]
    for copy in loads:
        copy.start()

    slots = slot[...]
    heat_row = ocean[0:16, :].astype(F32)[0:1]
    source = onehot(iota((DEVICES, OCN), 0) == slots // CAP)
    here = iota((128, OCN), 0) == slots % CAP + CAP * lax.rem(me, 4)
    values = jnp.concatenate([jnp.where(here, heat_row, 0.0).astype(BF), onehot(here)], axis=0)
    vsend[...] = dot_nt(source, values).reshape(8, 16, 256)

    pl.semaphore_wait(barrier, len(greeted))
    for step in range(1, 8):
        other = lax.rem(outer + step, 8)
        pltpu.make_async_remote_copy(
            src_ref=vsend.at[other], dst_ref=vfirst.at[outer], send_sem=a_send, recv_sem=a_recv,
            device_id=outer_peer(other), device_id_type=MESH,
        ).start()
    vfirst[outer] = vsend[outer]

    for copy in loads:
        copy.wait()
    sx[2 : AR + 2, :, 0:AC] = pltpu.einshape("crw->rcw", air_in[...])

    lane = iota((CH, 128), 1)

    def pack_row(row, carry):
        left, right = carry
        first = jnp.where(lane < 2, sx[row + 2, :, 0:128].astype(F32), 0.0)
        last = jnp.where(lane >= 126, sx[row + 2, :, AC - 128 : AC].astype(F32), 0.0)
        left = left + pltpu.roll(first, 2 * row, 1)
        right = right + pltpu.roll(last, 2 * row + 2, 1)
        return left, right

    zero = jnp.zeros((CH, 128), F32)
    left, right = lax.fori_loop(0, AR, pack_row, (zero, zero), unroll=6)
    cols[0] = left.astype(BF)
    cols[1] = right.astype(BF)

    def rim(number, src, dst, send, recv):
        return pltpu.make_async_remote_copy(
            src_ref=src, dst_ref=dst, send_sem=send.at[number], recv_sem=recv.at[number],
            device_id=around[number], device_id_type=MESH,
        )

    air_rims = [
        rim(0, sx.at[2:4, :, 0:AC], sx.at[AR + 2 : AR + 4, :, 0:AC], r_send, r_recv),
        rim(1, sx.at[AR : AR + 2, :, 0:AC], sx.at[0:2, :, 0:AC], r_send, r_recv),
        rim(2, cols.at[0], rcols.at[1], r_send, r_recv),
        rim(3, cols.at[1], rcols.at[0], r_send, r_recv),
        rim(4, cols.at[0], rcols.at[5], r_send, r_recv),
        rim(5, cols.at[0], rcols.at[3], r_send, r_recv),
        rim(6, cols.at[1], rcols.at[4], r_send, r_recv),
        rim(7, cols.at[1], rcols.at[2], r_send, r_recv),
    ]
    for copy in air_rims:
        copy.start()

    pltpu.make_async_copy(vfirst.at[pl.ds(0, 7)], vfirst.at[pl.ds(0, 7)], a_recv).wait()
    vturned[...] = pltpu.einshape("bal->abl", vfirst[...])
    for step in range(1, 16):
        other = lax.rem(inner_place + step, 16)
        pltpu.make_async_remote_copy(
            src_ref=vturned.at[other], dst_ref=vrecv.at[inner_place], send_sem=b_send, recv_sem=b_recv,
            device_id=inner_peer(other), device_id_type=MESH,
        ).start()
    vrecv[inner_place] = vturned[inner_place]

    def make_columns(step, carry):
        base = pl.multiple_of(step * 256, 256)
        column = cells[0:1, pl.ds(base, 256)] % AC
        onecol[:, pl.ds(base, 256)] = onehot(iota((AC, 256), 0) == column)
        return carry

    lax.fori_loop(0, SLOTS // 256, make_columns, 0, unroll=2)
    for number, weight in enumerate((w1_in, w2_in)):
        for row_tap in range(3):
            for col_tap in range(3):
                weights[number, row_tap * CH : (row_tap + 1) * CH, col_tap * CH : (col_tap + 1) * CH] = weight[
                    row_tap, col_tap
                ]
    for number, weight in enumerate((m1_in, m2_in)):
        for tap in range(TAPS):
            mweights[number, :, tap * CH : (tap + 1) * CH] = weight[tap]
    channel_weight = jnp.sum(
        jnp.where(iota((CH, CH), 0) == iota((CH, CH), 1), heat[...], 0.0), axis=1, keepdims=True
    )

    pltpu.make_async_copy(vrecv.at[pl.ds(0, 15)], vrecv.at[pl.ds(0, 15)], b_recv).wait()
    for quarter in range(4):
        four = vrecv[quarter * 4 : quarter * 4 + 4]
        lines = (four[0] + four[1]) + (four[2] + four[3])
        for part in range(8):
            base = (part * 4 + quarter) * 128
            hit = iota((CAP, 128), 0) == cells[0:1, base : base + 128] // AC
            for kind in range(2):
                picked_cols[CAP * kind : CAP * (kind + 1), base : base + 128] = jnp.where(
                    hit, lines[part : part + 1, kind * 128 : (kind + 1) * 128], 0.0
                ).astype(BF)
    sums = dot_nt(picked_cols[...], onecol[...])
    sst[8 : 8 + AR, 128 : 128 + AC] = sums[0:AR] / jnp.maximum(sums[CAP : CAP + AR], 1.0)

    top, low, far = 128, 640, 768
    sst_rims = [
        rim(0, sst.at[8:16, top:low], sst.at[32:40, top:low], s_send, s_recv),
        rim(1, sst.at[24:32, top:low], sst.at[0:8, top:low], s_send, s_recv),
        rim(2, sst.at[8:32, 128:256], sst.at[8:32, low:far], s_send, s_recv),
        rim(3, sst.at[8:32, 512:640], sst.at[8:32, 0:128], s_send, s_recv),
        rim(4, sst.at[8:16, 128:256], sst.at[32:40, low:far], s_send, s_recv),
        rim(5, sst.at[24:32, 128:256], sst.at[0:8, low:far], s_send, s_recv),
        rim(6, sst.at[8:16, 512:640], sst.at[32:40, 0:128], s_send, s_recv),
        rim(7, sst.at[24:32, 512:640], sst.at[0:8, 0:128], s_send, s_recv),
    ]
    for copy in sst_rims:
        copy.start()
    def begin(row, carry):
        line = sst[pl.ds(row + 8, 1), 128 : 128 + AC]
        state = sx[row + 2, :, 0:AC].astype(F32) + channel_weight * line
        sx[row + 2, :, 0:AC] = state.astype(BF)
        return carry

    for copy in air_rims:
        copy.wait()
    lax.fori_loop(0, AR, begin, 0, unroll=6)

    def ring_block(row, left, right):
        from_right = pltpu.roll(right, lax.rem(128 - 2 * row, 128), 1)
        from_left = pltpu.roll(left, lax.rem(254 - 2 * row, 128), 1)
        return jnp.where(lane < 64, from_right, from_left).astype(BF)

    def extend(row, carry):
        sx[row + 2, :, AC:RING] = ring_block(row, rcols[0].astype(F32), rcols[1].astype(F32))
        return carry

    lax.fori_loop(0, AR, extend, 0, unroll=6)
    for row in range(2):
        sx[row, :, AC:RING] = ring_block(jnp.int32(AR - 2 + row), rcols[2].astype(F32), rcols[3].astype(F32))
        sx[AR + 2 + row, :, AC:RING] = ring_block(jnp.int32(row), rcols[4].astype(F32), rcols[5].astype(F32))

    def make_taps(step, carry):
        base = pl.multiple_of(step * 256, 256)
        for tap in range(TAPS):
            inner = (taps_in[tap : tap + 1, pl.ds(base, 256)] - base) % 256
            onetap[tap, :, pl.ds(base, 256)] = onehot(iota((256, 256), 0) == inner)
        return carry

    lax.fori_loop(0, OCN // 256, make_taps, 0)

    for copy in sst_rims:
        copy.wait()

    low_lane = iota((1, 128), 1) < 64

    def begin_block(row, inside):
        whole = sst[pl.ds(row + 6, 1), :]
        line = jnp.where(low_lane, whole[:, 640:768], whole[:, 0:128])
        state = sx[row, :, AC:RING].astype(F32) + channel_weight * line
        sx[row, :, AC:RING] = jnp.where(inside, state, 0.0).astype(BF)

    def begin_side(row, carry):
        begin_block(row + 2, True)
        return carry

    lax.fori_loop(0, AR, begin_side, 0, unroll=6)
    for row in (0, 1, AR + 2, AR + 3):
        inside = tile > 0 if row < 2 else tile < TILES - 1
        state = sx[row, :, 0:AC].astype(F32) + channel_weight * sst[row + 6 : row + 7, 128 : 128 + AC]
        sx[row, :, 0:AC] = jnp.where(inside, state, 0.0).astype(BF)
        begin_block(row, inside)

    def three(x, width):
        west_of = pltpu.roll(x, 1, 1)[:, 0:width]
        east_of = pltpu.roll(x, RING - 1, 1)[:, 0:width]
        return jnp.concatenate([west_of, x[:, 0:width], east_of], axis=0)

    def first_conv(row, carry):
        part = dot(weights[0], three(sx[row], RING))
        total = acc[0] + part[2 * CH : 3 * CH]
        acc[0] = acc[1] + part[CH : 2 * CH]
        acc[1] = part[0:CH]
        middle = row - 2
        inside = jnp.logical_and(jnp.logical_or(middle >= 1, tile > 0), jnp.logical_or(middle < AR + 1, tile < TILES - 1))
        hidden = jnp.where(inside, jax.nn.gelu(total, approximate=True), 0.0)
        hx[jnp.maximum(middle, 0)] = hidden.astype(BF)
        return carry

    lax.fori_loop(0, AR + 4, first_conv, 0, unroll=AR + 4)

    def second_conv(row, carry):
        part = dot(weights[1], three(hx[row], AC))
        total = acc[0, :, 0:AC] + part[2 * CH : 3 * CH]
        acc[0, :, 0:AC] = acc[1, :, 0:AC] + part[CH : 2 * CH]
        acc[1, :, 0:AC] = part[0:CH]
        middle = jnp.maximum(row - 2, 0)
        after[middle] = (sx[middle + 2, :, 0:AC].astype(F32) + total).astype(BF)
        return carry

    lax.fori_loop(0, AR + 2, second_conv, 0, unroll=AR + 2)

    first_block = lax.div(me, 8)

    def block_of(step):
        return lax.rem(first_block + step, DEVICES // 8)

    def find(block):
        base = pl.multiple_of(block * 256, 256)
        row = cells[0:1, pl.ds(base, 256)] // AC
        select = onecol[:, pl.ds(base, 256)]
        state = jnp.zeros((CH, 256), F32)
        for part in range(AR // 4):
            rows = after[part * 4 : part * 4 + 4].reshape(4 * CH, AC)
            found = dot(rows, select)
            for inner in range(4):
                state = jnp.where(row == part * 4 + inner, found[inner * CH : (inner + 1) * CH], state)
        return state

    def ship(state, block, others):
        flat = jnp.transpose(state).reshape(8, CAP, CH)
        pair = jnp.concatenate([flat[:, 0:16], flat[:, 16:32]], axis=2)
        gsend[pl.ds(pl.multiple_of(block * 8, 8), 8)] = pair.astype(BF)
        for inner in others:
            other = block * 8 + inner
            pltpu.make_async_remote_copy(
                src_ref=gsend.at[other], dst_ref=grecv.at[me], send_sem=g_send, recv_sem=g_recv,
                device_id=where_of(other), device_id_type=MESH,
            ).start()

    def coupling(step, state):
        found = find(block_of(step))
        ship(state, block_of(step - 1), range(8))
        return found

    state = lax.fori_loop(2, DEVICES // 8 + 1, coupling, find(block_of(1)), unroll=3)
    ship(state, first_block, [lax.rem(me + step, 8) for step in range(1, 8)])
    grecv[me] = gsend[me]

    air_done[...] = pltpu.einshape("rcw->crw", after[...])
    store = pltpu.make_async_copy(air_done, air_out, local.at[0])
    store.start()

    def make_slots(step, carry):
        base = pl.multiple_of(step * 256, 256)
        mark = slot[0:1, pl.ds(base, 256)]
        row = mark // CAP * 16 + mark % 16

        def fill(part, inner_carry):
            first = pl.multiple_of(part * 256, 256)
            oneslot[pl.ds(first, 256), pl.ds(base, 256)] = onehot(iota((256, 256), 0) + first == row)
            return inner_carry

        return lax.fori_loop(0, OCN // 256, fill, carry)

    lax.fori_loop(0, OCN // 256, make_slots, 0)

    pltpu.make_async_copy(grecv.at[pl.ds(0, DEVICES - 1)], grecv.at[pl.ds(0, DEVICES - 1)], g_recv).wait()

    def turn(step, carry):
        eight = grecv[pl.ds(pl.multiple_of(step * 8, 8), 8)].reshape(128, 128)
        arrived[:, pl.ds(pl.multiple_of(step * 128, 128), 128)] = jnp.transpose(eight.astype(F32)).astype(BF)
        return carry

    lax.fori_loop(0, DEVICES // 8, turn, 0, unroll=8)

    def force(step, carry):
        base = pl.multiple_of(step * 256, 256)
        late = (slot[0:1, pl.ds(base, 256)] // 16) % 2 == 1
        found = dot(arrived[...], oneslot[:, pl.ds(base, 256)])
        forcing = jnp.where(late, found[CH : 2 * CH], found[0:CH])
        begun = ocean[:, pl.ds(base, 256)].astype(F32) + forcing
        window[:, pl.ds(base + HALO, 256)] = begun.astype(BF)
        return carry

    lax.fori_loop(0, OCN // 256, force, 0, unroll=4)

    previous = where_of(lax.rem(me + DEVICES - 1, DEVICES))
    following = where_of(lax.rem(me + 1, DEVICES))

    def ocean_rims(buffer, first):
        return [
            pltpu.make_async_remote_copy(
                src_ref=buffer.at[:, HALO : 2 * HALO], dst_ref=buffer.at[:, EXT - HALO : EXT],
                send_sem=o_send.at[first], recv_sem=o_recv.at[first], device_id=previous, device_id_type=MESH,
            ),
            pltpu.make_async_remote_copy(
                src_ref=buffer.at[:, OCN : OCN + HALO], dst_ref=buffer.at[:, 0:HALO],
                send_sem=o_send.at[first + 1], recv_sem=o_recv.at[first + 1], device_id=following, device_id_type=MESH,
            ),
        ]

    def mix(buffer, number, block):
        base = pl.multiple_of(block * 256, 256)
        segments = jnp.concatenate(
            [buffer[:, pl.ds(pl.multiple_of(base + 256 * part, 256), 256)] for part in range(3)], axis=0
        )
        groups = []
        for tap in range(TAPS):
            part_of = (taps_in[tap : tap + 1, pl.ds(base, 256)] - base) // 256
            found = dot(segments, onetap[tap, :, pl.ds(base, 256)])
            chosen = jnp.where(
                part_of == 0, found[0:CH], jnp.where(part_of == 1, found[CH : 2 * CH], found[2 * CH : 3 * CH])
            )
            groups.append(chosen.astype(BF))
        return dot(mweights[number], jnp.concatenate(groups, axis=0))

    def hidden_block(block):
        total = mix(window, 0, block)
        base = pl.multiple_of(block * 256, 256)
        hwindow[:, pl.ds(base + HALO, 256)] = jax.nn.gelu(total, approximate=True).astype(BF)

    def last_block(block):
        total = mix(hwindow, 1, block)
        base = pl.multiple_of(block * 256, 256)
        ocean_out[:, pl.ds(base, 256)] = (window[:, pl.ds(base + HALO, 256)].astype(F32) + total).astype(BF)

    def close_ends(buffer):
        @pl.when(me == 0)
        def _():
            buffer[:, 0:HALO] = jnp.zeros((CH, HALO), BF)

        @pl.when(me == DEVICES - 1)
        def _():
            buffer[:, EXT - HALO : EXT] = jnp.zeros((CH, HALO), BF)

    def layer(buffer, first, do_block):
        copies = ocean_rims(buffer, first)
        for copy in copies:
            copy.start()

        def middle(block, carry):
            do_block(block)
            return carry

        lax.fori_loop(1, 7, middle, 0, unroll=6)
        for copy in copies:
            copy.wait()
        close_ends(buffer)

        def ends(step, carry):
            do_block(step * 7)
            return carry

        lax.fori_loop(0, 2, ends, 0, unroll=2)

    layer(window, 0, hidden_block)
    layer(hwindow, 2, last_block)
    store.wait()

    pltpu.make_async_copy(vsend.at[pl.ds(0, 7)], vsend.at[pl.ds(0, 7)], a_send).wait()
    pltpu.make_async_copy(vturned.at[pl.ds(0, 15)], vturned.at[pl.ds(0, 15)], b_send).wait()
    pltpu.make_async_copy(gsend.at[pl.ds(0, DEVICES - 1)], gsend.at[pl.ds(0, DEVICES - 1)], g_send).wait()


def hand_over(air, ocean, air_out, ocean_out, air_held, ocean_held, come, go):
    pieces = [(ocean, ocean_held, ocean_out)]
    for part in range(4):
        rows = pl.ds(part * 16, 16)
        pieces.append((air.at[rows], air_held.at[rows], air_out.at[rows]))
    inward = [pltpu.make_async_copy(src, held, come.at[i]) for i, (src, held, _) in enumerate(pieces)]
    outward = [pltpu.make_async_copy(held, dst, go.at[i]) for i, (_, held, dst) in enumerate(pieces)]
    for copy in inward:
        copy.start()
    for first, second in zip(inward, outward):
        first.wait()
        second.start()
    for copy in outward:
        copy.wait()


def shards(atmos, ocean, heat, w1, w2, m1, m2, slot, cells, taps):
    vmem = pl.BlockSpec(memory_space=pltpu.VMEM)
    dma = pltpu.SemaphoreType.DMA
    anywhere = pl.BlockSpec(memory_space=pl.ANY)
    results = pl.pallas_call(
        kernel,
        out_shape=(
            jax.ShapeDtypeStruct((CH, AR, AC), BF),
            jax.ShapeDtypeStruct((CH, OCN), BF),
        ),
        in_specs=[anywhere, vmem, vmem] + [anywhere] * 4 + [vmem, vmem, anywhere],
        out_specs=(anywhere, vmem),
        scratch_shapes=[
            pltpu.VMEM((CH, AR, AC), BF),
            pltpu.VMEM((3, 3, CH, CH), BF),
            pltpu.VMEM((3, 3, CH, CH), BF),
            pltpu.VMEM((TAPS, CH, CH), BF),
            pltpu.VMEM((TAPS, CH, CH), BF),
            pltpu.VMEM((TAPS, OCN), I32),
            pltpu.VMEM((CH, AR, AC), BF),
            pltpu.VMEM((AR, CH, AC), BF),
            pltpu.VMEM((8, 16, 256), F32),
            pltpu.VMEM((8, 16, 256), F32),
            pltpu.VMEM((16, 8, 256), F32),
            pltpu.VMEM((16, 8, 256), F32),
            pltpu.VMEM((2, CH, 128), BF),
            pltpu.VMEM((6, CH, 128), BF),
            pltpu.VMEM((40, 768), F32),
            pltpu.VMEM((AR + 4, CH, RING), BF),
            pltpu.VMEM((AR + 2, CH, RING), BF),
            pltpu.VMEM((2, CH, RING), F32),
            pltpu.VMEM((2, 3 * CH, 3 * CH), BF),
            pltpu.VMEM((2 * CAP, SLOTS), BF),
            pltpu.VMEM((AC, SLOTS), BF),
            pltpu.VMEM((DEVICES, 16, 128), BF),
            pltpu.VMEM((DEVICES, 16, 128), BF),
            pltpu.VMEM((128, OCN), BF),
            pltpu.VMEM((OCN, OCN), BF),
            pltpu.VMEM((TAPS, 256, OCN), BF),
            pltpu.VMEM((2, CH, TAPS * CH), BF),
            pltpu.VMEM((CH, EXT), BF),
            pltpu.VMEM((CH, EXT), BF),
            dma((6,)), dma, dma, dma, dma, dma((8,)), dma((8,)), dma((8,)), dma((8,)), dma, dma, dma((4,)), dma((4,)),
        ],
        compiler_params=pltpu.CompilerParams(
            collective_id=0, has_side_effects=True, vmem_limit_bytes=56 << 20
        ),
        name="level",
    )(atmos, ocean, heat.reshape(1, CH), w1, w2, m1, m2, slot.reshape(1, OCN), cells, taps)
    return pl.pallas_call(
        hand_over,
        out_shape=(
            jax.ShapeDtypeStruct((CH, AR, AC), BF),
            jax.ShapeDtypeStruct((CH, OCN), BF),
        ),
        in_specs=[anywhere, anywhere],
        out_specs=(anywhere, anywhere),
        scratch_shapes=[pltpu.VMEM((CH, AR, AC), BF), pltpu.VMEM((CH, OCN), BF), dma((5,)), dma((5,))],
        name="hand_over",
    )(*results)


def solution(mesh):
    placed = (
        P(None, "tile", "face"),
        P(None, ("face", "tile")),
        P(),
        P(),
        P(),
        P(),
        P(),
        P(("face", "tile")),
        P(("face", "tile"), None),
        P(None, ("face", "tile")),
    )
    return jax.shard_map(
        shards,
        mesh=mesh,
        in_specs=placed,
        out_specs=(P(None, "tile", "face"), P(None, ("face", "tile"))),
        check_vma=False,
    )
```

```python
import jax
import jax.numpy as jnp
from jax import lax
from jax.experimental import pallas as pl
from jax.experimental.pallas import tpu as pltpu
from jax.sharding import PartitionSpec as P

MESH = pl.DeviceIdType.MESH
BF = jnp.bfloat16
F32 = jnp.float32
I32 = jnp.int32
FACES = 4
TILES = 32
DEVICES = 128
CAP = 32
CH = 64
AR = 24
AC = 512
OCN = 2048
SLOTS = 4096
HALO = 256
EXT = OCN + 2 * HALO
RING = AC + 128
TAPS = 9


def iota(shape, dim):
    return lax.broadcasted_iota(I32, shape, dim)


def dot(a, b):
    return jnp.dot(a, b, preferred_element_type=F32)


def dot_nt(a, b):
    return lax.dot_general(a, b, (((1,), (1,)), ((), ())), preferred_element_type=F32)


def onehot(mask):
    return jnp.where(mask, 1.0, 0.0).astype(BF)


def where_of(number):
    return (lax.div(number, TILES), lax.rem(number, TILES))


def kernel(
    air, ocean, heat, w1, w2, m1, m2, slot, cells, taps,
    air_out, ocean_out,
    air_in, w1_in, w2_in, m1_in, m2_in, taps_in, air_done, after,
    vsend, vrecv, cols, rcols, sst, sx, hx, acc, weights, picked_cols, onecol,
    gsend, grecv, arrived, oneslot, mweights, window, hwindow,
    local, entered, a_send, a_recv, r_send, r_recv, s_send, s_recv, g_send, g_recv, o_send, o_recv,
):
    face = lax.axis_index("face")
    tile = lax.axis_index("tile")
    me = face * TILES + tile

    outer = face * 2 + lax.div(tile, 16)
    inner_place = lax.rem(tile, 16)
    up = lax.rem(tile + TILES - 1, TILES)
    down = lax.rem(tile + 1, TILES)
    west = lax.rem(face + FACES - 1, FACES)
    east = lax.rem(face + 1, FACES)
    around = (
        (face, up), (face, down), (west, tile), (east, tile),
        (west, up), (west, down), (east, up), (east, down),
    )

    def outer_peer(number):
        return (lax.div(number, 2), lax.rem(number, 2) * 16 + inner_place)

    def inner_peer(number):
        return (face, lax.div(tile, 16) * 16 + number)

    barrier = pltpu.get_barrier_semaphore()
    near = [inner_peer(lax.rem(inner_place + step, 16)) for step in range(1, 16)]
    far = [outer_peer(lax.rem(outer + step, 8)) for step in range(1, 8)]
    for other in near + far:
        pl.semaphore_signal(barrier, inc=1, device_id=other, device_id_type=MESH)

    loads = [
        pltpu.make_async_copy(src, dst, local.at[number])
        for number, (src, dst) in enumerate(
            ((air, air_in), (w1, w1_in), (w2, w2_in), (m1, m1_in), (m2, m2_in), (taps, taps_in))
        )
    ]
    for copy in loads:
        copy.start()

    slots = slot[...]
    heat_row = ocean[0:16, :].astype(F32)[0:1]
    here = iota((128, OCN), 0) == slots % CAP + CAP * lax.rem(me, 4)
    values = jnp.concatenate([jnp.where(here, heat_row, 0.0).astype(BF), onehot(here)], axis=0)
    pl.semaphore_wait(barrier, len(near) + len(far))
    for other in near:
        pl.semaphore_signal(entered, inc=1, device_id=other, device_id_type=MESH)
    source = onehot(iota((DEVICES, OCN), 0) == slots // CAP)
    vsend[:, 0, :] = dot_nt(source, values)
    pl.semaphore_wait(entered, len(near))

    def send_values(step, carry):
        other = lax.rem(me + step, DEVICES)
        pltpu.make_async_remote_copy(
            src_ref=vsend.at[other], dst_ref=vrecv.at[me], send_sem=a_send, recv_sem=a_recv,
            device_id=where_of(other), device_id_type=MESH,
        ).start()
        return carry

    lax.fori_loop(1, DEVICES, send_values, 0)
    vrecv[me] = vsend[me]

    for copy in loads:
        copy.wait()
    sx[2 : AR + 2, :, 0:AC] = pltpu.einshape("crw->rcw", air_in[...])

    lane = iota((CH, 128), 1)

    def pack_row(row, carry):
        left, right = carry
        first = jnp.where(lane < 2, sx[row + 2, :, 0:128].astype(F32), 0.0)
        last = jnp.where(lane >= 126, sx[row + 2, :, AC - 128 : AC].astype(F32), 0.0)
        left = left + pltpu.roll(first, 2 * row, 1)
        right = right + pltpu.roll(last, 2 * row + 2, 1)
        return left, right

    zero = jnp.zeros((CH, 128), F32)
    left, right = lax.fori_loop(0, AR, pack_row, (zero, zero), unroll=6)
    cols[0] = left.astype(BF)
    cols[1] = right.astype(BF)

    def rim(number, src, dst, send, recv):
        return pltpu.make_async_remote_copy(
            src_ref=src, dst_ref=dst, send_sem=send.at[number], recv_sem=recv.at[number],
            device_id=around[number], device_id_type=MESH,
        )

    air_rims = [
        rim(0, sx.at[2:4, :, 0:AC], sx.at[AR + 2 : AR + 4, :, 0:AC], r_send, r_recv),
        rim(1, sx.at[AR : AR + 2, :, 0:AC], sx.at[0:2, :, 0:AC], r_send, r_recv),
        rim(2, cols.at[0], rcols.at[1], r_send, r_recv),
        rim(3, cols.at[1], rcols.at[0], r_send, r_recv),
        rim(4, cols.at[0], rcols.at[5], r_send, r_recv),
        rim(5, cols.at[0], rcols.at[3], r_send, r_recv),
        rim(6, cols.at[1], rcols.at[4], r_send, r_recv),
        rim(7, cols.at[1], rcols.at[2], r_send, r_recv),
    ]
    for copy in air_rims:
        copy.start()

    def make_columns(step, carry):
        base = pl.multiple_of(step * 256, 256)
        column = cells[0:1, pl.ds(base, 256)] % AC
        onecol[:, pl.ds(base, 256)] = onehot(iota((AC, 256), 0) == column)
        return carry

    lax.fori_loop(0, SLOTS // 256, make_columns, 0, unroll=2)
    for number, weight in enumerate((w1_in, w2_in)):
        for row_tap in range(3):
            for col_tap in range(3):
                weights[number, row_tap * CH : (row_tap + 1) * CH, col_tap * CH : (col_tap + 1) * CH] = weight[
                    row_tap, col_tap
                ]
    for number, weight in enumerate((m1_in, m2_in)):
        for tap in range(TAPS):
            mweights[number, :, tap * CH : (tap + 1) * CH] = weight[tap]
    channel_weight = jnp.sum(
        jnp.where(iota((CH, CH), 0) == iota((CH, CH), 1), heat[...], 0.0), axis=1, keepdims=True
    )

    pltpu.make_async_copy(vrecv.at[pl.ds(0, DEVICES - 1)], vrecv.at[pl.ds(0, DEVICES - 1)], a_recv).wait()
    for block in range(SLOTS // 128):
        base = block * 128
        line = (vrecv[4 * block] + vrecv[4 * block + 1]) + (vrecv[4 * block + 2] + vrecv[4 * block + 3])
        hit = iota((CAP, 128), 0) == cells[0:1, base : base + 128] // AC
        for kind in range(2):
            picked_cols[CAP * kind : CAP * (kind + 1), base : base + 128] = jnp.where(
                hit, line[:, kind * 128 : (kind + 1) * 128], 0.0
            ).astype(BF)
    sums = dot_nt(picked_cols[...], onecol[...])
    sst[8 : 8 + AR, 128 : 128 + AC] = sums[0:AR] / jnp.maximum(sums[CAP : CAP + AR], 1.0)

    top, low, far = 128, 640, 768
    sst_rims = [
        rim(0, sst.at[8:16, top:low], sst.at[32:40, top:low], s_send, s_recv),
        rim(1, sst.at[24:32, top:low], sst.at[0:8, top:low], s_send, s_recv),
        rim(2, sst.at[8:32, 128:256], sst.at[8:32, low:far], s_send, s_recv),
        rim(3, sst.at[8:32, 512:640], sst.at[8:32, 0:128], s_send, s_recv),
        rim(4, sst.at[8:16, 128:256], sst.at[32:40, low:far], s_send, s_recv),
        rim(5, sst.at[24:32, 128:256], sst.at[0:8, low:far], s_send, s_recv),
        rim(6, sst.at[8:16, 512:640], sst.at[32:40, 0:128], s_send, s_recv),
        rim(7, sst.at[24:32, 512:640], sst.at[0:8, 0:128], s_send, s_recv),
    ]
    for copy in sst_rims:
        copy.start()
    def begin(row, carry):
        line = sst[pl.ds(row + 8, 1), 128 : 128 + AC]
        state = sx[row + 2, :, 0:AC].astype(F32) + channel_weight * line
        sx[row + 2, :, 0:AC] = state.astype(BF)
        return carry

    for copy in air_rims:
        copy.wait()
    lax.fori_loop(0, AR, begin, 0, unroll=6)

    def ring_block(row, left, right):
        from_right = pltpu.roll(right, lax.rem(128 - 2 * row, 128), 1)
        from_left = pltpu.roll(left, lax.rem(254 - 2 * row, 128), 1)
        return jnp.where(lane < 64, from_right, from_left).astype(BF)

    def extend(row, carry):
        sx[row + 2, :, AC:RING] = ring_block(row, rcols[0].astype(F32), rcols[1].astype(F32))
        return carry

    lax.fori_loop(0, AR, extend, 0, unroll=6)
    for row in range(2):
        sx[row, :, AC:RING] = ring_block(jnp.int32(AR - 2 + row), rcols[2].astype(F32), rcols[3].astype(F32))
        sx[AR + 2 + row, :, AC:RING] = ring_block(jnp.int32(row), rcols[4].astype(F32), rcols[5].astype(F32))

    for copy in sst_rims:
        copy.wait()

    low_lane = iota((1, 128), 1) < 64

    def begin_block(row, inside):
        whole = sst[pl.ds(row + 6, 1), :]
        line = jnp.where(low_lane, whole[:, 640:768], whole[:, 0:128])
        state = sx[row, :, AC:RING].astype(F32) + channel_weight * line
        sx[row, :, AC:RING] = jnp.where(inside, state, 0.0).astype(BF)

    def begin_side(row, carry):
        begin_block(row + 2, True)
        return carry

    lax.fori_loop(0, AR, begin_side, 0, unroll=6)
    for row in (0, 1, AR + 2, AR + 3):
        inside = tile > 0 if row < 2 else tile < TILES - 1
        state = sx[row, :, 0:AC].astype(F32) + channel_weight * sst[row + 6 : row + 7, 128 : 128 + AC]
        sx[row, :, 0:AC] = jnp.where(inside, state, 0.0).astype(BF)
        begin_block(row, inside)

    def three(x, width):
        west_of = pltpu.roll(x, 1, 1)[:, 0:width]
        east_of = pltpu.roll(x, RING - 1, 1)[:, 0:width]
        return jnp.concatenate([west_of, x[:, 0:width], east_of], axis=0)

    def first_conv(row, carry):
        part = dot(weights[0], three(sx[row], RING))
        total = acc[0] + part[2 * CH : 3 * CH]
        acc[0] = acc[1] + part[CH : 2 * CH]
        acc[1] = part[0:CH]
        middle = row - 2
        inside = jnp.logical_and(jnp.logical_or(middle >= 1, tile > 0), jnp.logical_or(middle < AR + 1, tile < TILES - 1))
        hidden = jnp.where(inside, jax.nn.gelu(total, approximate=True), 0.0)
        hx[jnp.maximum(middle, 0)] = hidden.astype(BF)
        return carry

    lax.fori_loop(0, AR + 4, first_conv, 0, unroll=7)

    def second_conv(row, carry):
        part = dot(weights[1], three(hx[row], AC))
        total = acc[0, :, 0:AC] + part[2 * CH : 3 * CH]
        acc[0, :, 0:AC] = acc[1, :, 0:AC] + part[CH : 2 * CH]
        acc[1, :, 0:AC] = part[0:CH]
        middle = jnp.maximum(row - 2, 0)
        after[middle] = (sx[middle + 2, :, 0:AC].astype(F32) + total).astype(BF)
        return carry

    lax.fori_loop(0, AR + 2, second_conv, 0, unroll=13)

    first_block = lax.div(me, 8)

    def block_of(step):
        return lax.rem(first_block + step, DEVICES // 8)

    def find(block):
        base = pl.multiple_of(block * 256, 256)
        row = cells[0:1, pl.ds(base, 256)] // AC
        select = onecol[:, pl.ds(base, 256)]
        state = jnp.zeros((CH, 256), F32)
        for part in range(AR // 4):
            rows = after[part * 4 : part * 4 + 4].reshape(4 * CH, AC)
            found = dot(rows, select)
            for inner in range(4):
                state = jnp.where(row == part * 4 + inner, found[inner * CH : (inner + 1) * CH], state)
        return state

    def ship(state, block, others):
        flat = jnp.transpose(state).reshape(8, CAP, CH)
        pair = jnp.concatenate([flat[:, 0:16], flat[:, 16:32]], axis=2)
        gsend[pl.ds(pl.multiple_of(block * 8, 8), 8)] = pair.astype(BF)
        for inner in others:
            other = block * 8 + inner
            pltpu.make_async_remote_copy(
                src_ref=gsend.at[other], dst_ref=grecv.at[me], send_sem=g_send, recv_sem=g_recv,
                device_id=where_of(other), device_id_type=MESH,
            ).start()

    def coupling(step, state):
        found = find(block_of(step))
        ship(state, block_of(step - 1), range(8))
        return found

    state = lax.fori_loop(2, DEVICES // 8 + 1, coupling, find(block_of(1)), unroll=3)
    ship(state, first_block, [lax.rem(me + step, 8) for step in range(1, 8)])
    grecv[me] = gsend[me]

    air_done[...] = pltpu.einshape("rcw->crw", after[...])
    store = pltpu.make_async_copy(air_done, air_out, local.at[0])
    store.start()

    def make_slots(step, carry):
        base = pl.multiple_of(step * 256, 256)
        mark = slot[0:1, pl.ds(base, 256)]
        row = mark // CAP * 16 + mark % 16

        def fill(part, inner_carry):
            first = pl.multiple_of(part * 256, 256)
            oneslot[pl.ds(first, 256), pl.ds(base, 256)] = onehot(iota((256, 256), 0) + first == row)
            return inner_carry

        return lax.fori_loop(0, OCN // 256, fill, carry)

    lax.fori_loop(0, OCN // 256, make_slots, 0)

    pltpu.make_async_copy(grecv.at[pl.ds(0, DEVICES - 1)], grecv.at[pl.ds(0, DEVICES - 1)], g_recv).wait()

    def turn(step, carry):
        eight = grecv[pl.ds(pl.multiple_of(step * 8, 8), 8)].reshape(128, 128)
        arrived[:, pl.ds(pl.multiple_of(step * 128, 128), 128)] = jnp.transpose(eight.astype(F32)).astype(BF)
        return carry

    lax.fori_loop(0, DEVICES // 8, turn, 0, unroll=8)

    def force(step, carry):
        base = pl.multiple_of(step * 256, 256)
        late = (slot[0:1, pl.ds(base, 256)] // 16) % 2 == 1
        found = dot(arrived[...], oneslot[:, pl.ds(base, 256)])
        forcing = jnp.where(late, found[CH : 2 * CH], found[0:CH])
        begun = ocean[:, pl.ds(base, 256)].astype(F32) + forcing
        window[:, pl.ds(base + HALO, 256)] = begun.astype(BF)
        return carry

    lax.fori_loop(0, OCN // 256, force, 0, unroll=4)

    previous = where_of(lax.rem(me + DEVICES - 1, DEVICES))
    following = where_of(lax.rem(me + 1, DEVICES))

    def ocean_rims(buffer, first):
        return [
            pltpu.make_async_remote_copy(
                src_ref=buffer.at[:, HALO : 2 * HALO], dst_ref=buffer.at[:, EXT - HALO : EXT],
                send_sem=o_send.at[first], recv_sem=o_recv.at[first], device_id=previous, device_id_type=MESH,
            ),
            pltpu.make_async_remote_copy(
                src_ref=buffer.at[:, OCN : OCN + HALO], dst_ref=buffer.at[:, 0:HALO],
                send_sem=o_send.at[first + 1], recv_sem=o_recv.at[first + 1], device_id=following, device_id_type=MESH,
            ),
        ]

    def mix(buffer, number, block):
        base = pl.multiple_of(block * 256, 256)
        segments = jnp.concatenate(
            [buffer[:, pl.ds(pl.multiple_of(base + 256 * part, 256), 256)] for part in range(3)], axis=0
        )
        groups = []
        for tap in range(TAPS):
            index = taps_in[tap : tap + 1, pl.ds(base, 256)] - base
            part_of = index // 256
            found = dot(segments, onehot(iota((256, 256), 0) == index % 256))
            chosen = jnp.where(
                part_of == 0, found[0:CH], jnp.where(part_of == 1, found[CH : 2 * CH], found[2 * CH : 3 * CH])
            )
            groups.append(chosen.astype(BF))
        return dot(mweights[number], jnp.concatenate(groups, axis=0))

    def hidden_block(block):
        total = mix(window, 0, block)
        base = pl.multiple_of(block * 256, 256)
        hwindow[:, pl.ds(base + HALO, 256)] = jax.nn.gelu(total, approximate=True).astype(BF)

    def last_block(block):
        total = mix(hwindow, 1, block)
        base = pl.multiple_of(block * 256, 256)
        ocean_out[:, pl.ds(base, 256)] = (window[:, pl.ds(base + HALO, 256)].astype(F32) + total).astype(BF)

    def close_ends(buffer):
        @pl.when(me == 0)
        def _():
            buffer[:, 0:HALO] = jnp.zeros((CH, HALO), BF)

        @pl.when(me == DEVICES - 1)
        def _():
            buffer[:, EXT - HALO : EXT] = jnp.zeros((CH, HALO), BF)

    def layer(buffer, first, do_block):
        copies = ocean_rims(buffer, first)
        for copy in copies:
            copy.start()

        def middle(block, carry):
            do_block(block)
            return carry

        lax.fori_loop(1, 7, middle, 0, unroll=2)
        for copy in copies:
            copy.wait()
        close_ends(buffer)

        def ends(step, carry):
            do_block(step * 7)
            return carry

        lax.fori_loop(0, 2, ends, 0, unroll=2)

    layer(window, 0, hidden_block)
    layer(hwindow, 2, last_block)
    store.wait()

    pltpu.make_async_copy(vsend.at[pl.ds(0, DEVICES - 1)], vsend.at[pl.ds(0, DEVICES - 1)], a_send).wait()
    pltpu.make_async_copy(gsend.at[pl.ds(0, DEVICES - 1)], gsend.at[pl.ds(0, DEVICES - 1)], g_send).wait()


def hand_over(air, ocean, air_out, ocean_out, air_held, ocean_held, come, go):
    pieces = [(ocean, ocean_held, ocean_out)]
    for part in range(4):
        rows = pl.ds(part * 16, 16)
        pieces.append((air.at[rows], air_held.at[rows], air_out.at[rows]))
    inward = [pltpu.make_async_copy(src, held, come.at[i]) for i, (src, held, _) in enumerate(pieces)]
    outward = [pltpu.make_async_copy(held, dst, go.at[i]) for i, (_, held, dst) in enumerate(pieces)]
    for copy in inward:
        copy.start()
    for first, second in zip(inward, outward):
        first.wait()
        second.start()
    for copy in outward:
        copy.wait()


def shards(atmos, ocean, heat, w1, w2, m1, m2, slot, cells, taps):
    vmem = pl.BlockSpec(memory_space=pltpu.VMEM)
    dma = pltpu.SemaphoreType.DMA
    anywhere = pl.BlockSpec(memory_space=pl.ANY)
    results = pl.pallas_call(
        kernel,
        out_shape=(
            jax.ShapeDtypeStruct((CH, AR, AC), BF),
            jax.ShapeDtypeStruct((CH, OCN), BF),
        ),
        in_specs=[anywhere, vmem, vmem] + [anywhere] * 4 + [vmem, vmem, anywhere],
        out_specs=(anywhere, vmem),
        scratch_shapes=[
            pltpu.VMEM((CH, AR, AC), BF),
            pltpu.VMEM((3, 3, CH, CH), BF),
            pltpu.VMEM((3, 3, CH, CH), BF),
            pltpu.VMEM((TAPS, CH, CH), BF),
            pltpu.VMEM((TAPS, CH, CH), BF),
            pltpu.VMEM((TAPS, OCN), I32),
            pltpu.VMEM((CH, AR, AC), BF),
            pltpu.VMEM((AR, CH, AC), BF),
            pltpu.VMEM((DEVICES, 1, 256), F32),
            pltpu.VMEM((DEVICES, 1, 256), F32),
            pltpu.VMEM((2, CH, 128), BF),
            pltpu.VMEM((6, CH, 128), BF),
            pltpu.VMEM((40, 768), F32),
            pltpu.VMEM((AR + 4, CH, RING), BF),
            pltpu.VMEM((AR + 2, CH, RING), BF),
            pltpu.VMEM((2, CH, RING), F32),
            pltpu.VMEM((2, 3 * CH, 3 * CH), BF),
            pltpu.VMEM((2 * CAP, SLOTS), BF),
            pltpu.VMEM((AC, SLOTS), BF),
            pltpu.VMEM((DEVICES, 16, 128), BF),
            pltpu.VMEM((DEVICES, 16, 128), BF),
            pltpu.VMEM((128, OCN), BF),
            pltpu.VMEM((OCN, OCN), BF),
            pltpu.VMEM((2, CH, TAPS * CH), BF),
            pltpu.VMEM((CH, EXT), BF),
            pltpu.VMEM((CH, EXT), BF),
            dma((6,)), pltpu.SemaphoreType.REGULAR, dma, dma, dma((8,)), dma((8,)), dma((8,)), dma((8,)), dma, dma, dma((4,)), dma((4,)),
        ],
        compiler_params=pltpu.CompilerParams(
            collective_id=0, has_side_effects=True, vmem_limit_bytes=56 << 20
        ),
        name="level",
    )(atmos, ocean, heat.reshape(1, CH), w1, w2, m1, m2, slot.reshape(1, OCN), cells, taps)
    return pl.pallas_call(
        hand_over,
        out_shape=(
            jax.ShapeDtypeStruct((CH, AR, AC), BF),
            jax.ShapeDtypeStruct((CH, OCN), BF),
        ),
        in_specs=[anywhere, anywhere],
        out_specs=(anywhere, anywhere),
        scratch_shapes=[pltpu.VMEM((CH, AR, AC), BF), pltpu.VMEM((CH, OCN), BF), dma((5,)), dma((5,))],
        name="hand_over",
    )(*results)


def solution(mesh):
    placed = (
        P(None, "tile", "face"),
        P(None, ("face", "tile")),
        P(),
        P(),
        P(),
        P(),
        P(),
        P(("face", "tile")),
        P(("face", "tile"), None),
        P(None, ("face", "tile")),
    )
    return jax.shard_map(
        shards,
        mesh=mesh,
        in_specs=placed,
        out_specs=(P(None, "tile", "face"), P(None, ("face", "tile"))),
        check_vma=False,
    )
```

```python
import jax
import jax.numpy as jnp
from jax import lax
from jax.experimental import pallas as pl
from jax.experimental.pallas import tpu as pltpu
from jax.sharding import PartitionSpec as P

MESH = pl.DeviceIdType.MESH
BF = jnp.bfloat16
F32 = jnp.float32
I32 = jnp.int32
FACES = 4
TILES = 32
DEVICES = 128
CAP = 32
CH = 64
AR = 24
AC = 512
OCN = 2048
SLOTS = 4096
HALO = 256
EXT = OCN + 2 * HALO
RING = AC + 128
TAPS = 9


def iota(shape, dim):
    return lax.broadcasted_iota(I32, shape, dim)


def dot(a, b):
    return jnp.dot(a, b, preferred_element_type=F32)


def dot_nt(a, b):
    return lax.dot_general(a, b, (((1,), (1,)), ((), ())), preferred_element_type=F32)


def onehot(mask):
    return jnp.where(mask, 1.0, 0.0).astype(BF)


def where_of(number):
    return (lax.div(number, TILES), lax.rem(number, TILES))


def kernel(
    air, ocean_hbm, heat_hbm, w1, w2, m1, m2, slot_hbm, cells_hbm, taps,
    air_out, ocean_out,
    ocean, heat, slot, cells, ocean_done,
    air_in, w1_in, w2_in, m1_in, m2_in, taps_in, air_done, after,
    vsend, vrecv, cols, rcols, sst, sx, hx, acc, weights, picked_cols, onecol,
    gsend, grecv, arrived, landed, oneslot, mweights, window, hwindow,
    local, a_send, a_recv, r_send, r_recv, s_send, s_recv, g_send, g_recv, o_send, o_recv,
):
    face = lax.axis_index("face")
    tile = lax.axis_index("tile")
    me = face * TILES + tile

    up = lax.rem(tile + TILES - 1, TILES)
    down = lax.rem(tile + 1, TILES)
    west = lax.rem(face + FACES - 1, FACES)
    east = lax.rem(face + 1, FACES)
    around = (
        (face, up), (face, down), (west, tile), (east, tile),
        (west, up), (west, down), (east, up), (east, down),
    )

    loads = [
        pltpu.make_async_copy(src, dst, local.at[number])
        for number, (src, dst) in enumerate(
            (
                (slot_hbm, slot), (ocean_hbm, ocean), (cells_hbm, cells), (heat_hbm, heat), (air, air_in),
                (w1, w1_in), (w2, w2_in), (m1, m1_in), (m2, m2_in), (taps, taps_in),
            )
        )
    ]
    for copy in loads:
        copy.start()

    barrier = pltpu.get_barrier_semaphore()

    def greet(step, carry):
        pl.semaphore_signal(
            barrier, inc=1, device_id=where_of(lax.rem(me + step, DEVICES)), device_id_type=MESH
        )
        return carry

    lax.fori_loop(0, 42, lambda step, carry: greet(3 * step + 3, greet(3 * step + 2, greet(3 * step + 1, carry))), 0)
    greet(127, 0)

    for copy in loads[:2]:
        copy.wait()

    slots = slot[...]
    heat_row = ocean[0:16, :].astype(F32)[0:1]
    here = iota((128, OCN), 0) == slots % CAP + CAP * lax.rem(me, 4)
    values = jnp.concatenate([jnp.where(here, heat_row, 0.0).astype(BF), onehot(here)], axis=0)
    source = onehot(iota((DEVICES, OCN), 0) == slots // CAP)
    vsend[:, 0, :] = dot_nt(source, values)
    pl.semaphore_wait(barrier, DEVICES - 1)

    def send_values(step, carry):
        other = lax.rem(me + step, DEVICES)
        pltpu.make_async_remote_copy(
            src_ref=vsend.at[other], dst_ref=vrecv.at[me], send_sem=a_send, recv_sem=a_recv,
            device_id=where_of(other), device_id_type=MESH,
        ).start()
        return carry

    lax.fori_loop(0, 42, lambda step, carry: send_values(3 * step + 3, send_values(3 * step + 2, send_values(3 * step + 1, carry))), 0)
    send_values(127, 0)
    vrecv[me] = vsend[me]

    for copy in loads[2:]:
        copy.wait()
    sx[2 : AR + 2, :, 0:AC] = pltpu.einshape("crw->rcw", air_in[...])

    lane = iota((CH, 128), 1)

    def pack_row(row, carry):
        left, right = carry
        first = jnp.where(lane < 2, sx[row + 2, :, 0:128].astype(F32), 0.0)
        last = jnp.where(lane >= 126, sx[row + 2, :, AC - 128 : AC].astype(F32), 0.0)
        left = left + pltpu.roll(first, 2 * row, 1)
        right = right + pltpu.roll(last, 2 * row + 2, 1)
        return left, right

    zero = jnp.zeros((CH, 128), F32)
    left, right = lax.fori_loop(0, AR, pack_row, (zero, zero), unroll=6)
    cols[0] = left.astype(BF)
    cols[1] = right.astype(BF)

    def rim(number, src, dst, send, recv):
        return pltpu.make_async_remote_copy(
            src_ref=src, dst_ref=dst, send_sem=send.at[number], recv_sem=recv.at[number],
            device_id=around[number], device_id_type=MESH,
        )

    air_rims = [
        rim(0, sx.at[2:4, :, 0:AC], sx.at[AR + 2 : AR + 4, :, 0:AC], r_send, r_recv),
        rim(1, sx.at[AR : AR + 2, :, 0:AC], sx.at[0:2, :, 0:AC], r_send, r_recv),
        rim(2, cols.at[0], rcols.at[1], r_send, r_recv),
        rim(3, cols.at[1], rcols.at[0], r_send, r_recv),
        rim(4, cols.at[0], rcols.at[5], r_send, r_recv),
        rim(5, cols.at[0], rcols.at[3], r_send, r_recv),
        rim(6, cols.at[1], rcols.at[4], r_send, r_recv),
        rim(7, cols.at[1], rcols.at[2], r_send, r_recv),
    ]
    for copy in air_rims:
        copy.start()

    def make_columns(step, carry):
        base = pl.multiple_of(step * 256, 256)
        column = cells[0:1, pl.ds(base, 256)] % AC
        onecol[:, pl.ds(base, 256)] = onehot(iota((AC, 256), 0) == column)
        return carry

    lax.fori_loop(0, SLOTS // 256, make_columns, 0, unroll=2)
    for number, weight in enumerate((w1_in, w2_in)):
        for row_tap in range(3):
            for col_tap in range(3):
                weights[number, row_tap * CH : (row_tap + 1) * CH, col_tap * CH : (col_tap + 1) * CH] = weight[
                    row_tap, col_tap
                ]
    for number, weight in enumerate((m1_in, m2_in)):
        for tap in range(TAPS):
            mweights[number, :, tap * CH : (tap + 1) * CH] = weight[tap]
    def make_slots(step, carry):
        base = pl.multiple_of(step * 256, 256)
        mark = slot[0:1, pl.ds(base, 256)]
        row = mark // CAP * 16 + mark % 16

        def fill(part, inner_carry):
            first = pl.multiple_of(part * 256, 256)
            oneslot[pl.ds(first, 256), pl.ds(base, 256)] = onehot(iota((256, 256), 0) + first == row)
            return inner_carry

        return lax.fori_loop(0, OCN // 256, fill, carry)

    lax.fori_loop(0, OCN // 256, make_slots, 0)

    channel_weight = jnp.sum(
        jnp.where(iota((CH, CH), 0) == iota((CH, CH), 1), heat[...], 0.0), axis=1, keepdims=True
    )

    pltpu.make_async_copy(vrecv.at[pl.ds(0, DEVICES - 1)], vrecv.at[pl.ds(0, DEVICES - 1)], a_recv).wait()
    for block in range(SLOTS // 128):
        base = block * 128
        line = (vrecv[4 * block] + vrecv[4 * block + 1]) + (vrecv[4 * block + 2] + vrecv[4 * block + 3])
        hit = iota((CAP, 128), 0) == cells[0:1, base : base + 128] // AC
        for kind in range(2):
            picked_cols[CAP * kind : CAP * (kind + 1), base : base + 128] = jnp.where(
                hit, line[:, kind * 128 : (kind + 1) * 128], 0.0
            ).astype(BF)
    sums = dot_nt(picked_cols[...], onecol[...])
    sst[8 : 8 + AR, 128 : 128 + AC] = sums[0:AR] / jnp.maximum(sums[CAP : CAP + AR], 1.0)

    top, low, far = 128, 640, 768
    sst_rims = [
        rim(0, sst.at[8:16, top:low], sst.at[32:40, top:low], s_send, s_recv),
        rim(1, sst.at[24:32, top:low], sst.at[0:8, top:low], s_send, s_recv),
        rim(2, sst.at[8:32, 128:256], sst.at[8:32, low:far], s_send, s_recv),
        rim(3, sst.at[8:32, 512:640], sst.at[8:32, 0:128], s_send, s_recv),
        rim(4, sst.at[8:16, 128:256], sst.at[32:40, low:far], s_send, s_recv),
        rim(5, sst.at[24:32, 128:256], sst.at[0:8, low:far], s_send, s_recv),
        rim(6, sst.at[8:16, 512:640], sst.at[32:40, 0:128], s_send, s_recv),
        rim(7, sst.at[24:32, 512:640], sst.at[0:8, 0:128], s_send, s_recv),
    ]
    for copy in sst_rims:
        copy.start()
    def begin(row, carry):
        line = sst[pl.ds(row + 8, 1), 128 : 128 + AC]
        state = sx[row + 2, :, 0:AC].astype(F32) + channel_weight * line
        sx[row + 2, :, 0:AC] = state.astype(BF)
        return carry

    for copy in air_rims:
        copy.wait()
    lax.fori_loop(0, AR, begin, 0, unroll=6)

    def ring_block(row, left, right):
        from_right = pltpu.roll(right, lax.rem(128 - 2 * row, 128), 1)
        from_left = pltpu.roll(left, lax.rem(254 - 2 * row, 128), 1)
        return jnp.where(lane < 64, from_right, from_left).astype(BF)

    def extend(row, carry):
        sx[row + 2, :, AC:RING] = ring_block(row, rcols[0].astype(F32), rcols[1].astype(F32))
        return carry

    lax.fori_loop(0, AR, extend, 0, unroll=6)
    for row in range(2):
        sx[row, :, AC:RING] = ring_block(jnp.int32(AR - 2 + row), rcols[2].astype(F32), rcols[3].astype(F32))
        sx[AR + 2 + row, :, AC:RING] = ring_block(jnp.int32(row), rcols[4].astype(F32), rcols[5].astype(F32))

    for copy in sst_rims:
        copy.wait()

    low_lane = iota((1, 128), 1) < 64

    def begin_block(row, inside):
        whole = sst[pl.ds(row + 6, 1), :]
        line = jnp.where(low_lane, whole[:, 640:768], whole[:, 0:128])
        state = sx[row, :, AC:RING].astype(F32) + channel_weight * line
        sx[row, :, AC:RING] = jnp.where(inside, state, 0.0).astype(BF)

    def begin_side(row, carry):
        begin_block(row + 2, True)
        return carry

    lax.fori_loop(0, AR, begin_side, 0, unroll=6)
    for row in (0, 1, AR + 2, AR + 3):
        inside = tile > 0 if row < 2 else tile < TILES - 1
        state = sx[row, :, 0:AC].astype(F32) + channel_weight * sst[row + 6 : row + 7, 128 : 128 + AC]
        sx[row, :, 0:AC] = jnp.where(inside, state, 0.0).astype(BF)
        begin_block(row, inside)

    def three(x, width):
        west_of = pltpu.roll(x, 1, 1)[:, 0:width]
        east_of = pltpu.roll(x, RING - 1, 1)[:, 0:width]
        return jnp.concatenate([west_of, x[:, 0:width], east_of], axis=0)

    def first_conv(row, carry):
        part = dot(weights[0], three(sx[row], RING))
        total = acc[0] + part[2 * CH : 3 * CH]
        acc[0] = acc[1] + part[CH : 2 * CH]
        acc[1] = part[0:CH]
        middle = row - 2
        inside = jnp.logical_and(jnp.logical_or(middle >= 1, tile > 0), jnp.logical_or(middle < AR + 1, tile < TILES - 1))
        hidden = jnp.where(inside, jax.nn.gelu(total, approximate=True), 0.0)
        hx[jnp.maximum(middle, 0)] = hidden.astype(BF)
        return carry

    lax.fori_loop(0, AR + 4, first_conv, 0, unroll=7)

    def second_conv(row, carry):
        part = dot(weights[1], three(hx[row], AC))
        total = acc[0, :, 0:AC] + part[2 * CH : 3 * CH]
        acc[0, :, 0:AC] = acc[1, :, 0:AC] + part[CH : 2 * CH]
        acc[1, :, 0:AC] = part[0:CH]
        middle = jnp.maximum(row - 2, 0)
        after[middle] = (sx[middle + 2, :, 0:AC].astype(F32) + total).astype(BF)
        return carry

    lax.fori_loop(0, AR + 2, second_conv, 0, unroll=13)

    first_block = lax.div(me, 8)

    def block_of(step):
        return lax.rem(first_block + step, DEVICES // 8)

    def find(block):
        base = pl.multiple_of(block * 256, 256)
        row = cells[0:1, pl.ds(base, 256)] // AC
        select = onecol[:, pl.ds(base, 256)]
        state = jnp.zeros((CH, 256), F32)
        for part in range(AR // 4):
            rows = after[part * 4 : part * 4 + 4].reshape(4 * CH, AC)
            found = dot(rows, select)
            for inner in range(4):
                state = jnp.where(row == part * 4 + inner, found[inner * CH : (inner + 1) * CH], state)
        return state

    def ship(state, block, others, number):
        flat = jnp.transpose(state).reshape(8, CAP, CH)
        pair = jnp.concatenate([flat[:, 0:16], flat[:, 16:32]], axis=2)
        gsend[pl.ds(pl.multiple_of(block * 8, 8), 8)] = pair.astype(BF)
        for inner in others:
            other = block * 8 + inner
            pltpu.make_async_remote_copy(
                src_ref=gsend.at[other], dst_ref=grecv.at[me], send_sem=g_send, recv_sem=g_recv.at[number],
                device_id=where_of(other), device_id_type=MESH,
            ).start()

    def coupling(step, state):
        found = find(block_of(step))
        ship(state, block_of(step - 1), range(8), lax.div(step - 2, 4))
        return found

    state = lax.fori_loop(2, DEVICES // 8 + 1, coupling, find(block_of(1)), unroll=3)
    ship(state, first_block, [lax.rem(me + step, 8) for step in range(1, 8)], 3)
    grecv[me] = gsend[me]

    air_done[...] = pltpu.einshape("rcw->crw", after[...])
    store = pltpu.make_async_copy(air_done, air_out, local.at[0])
    store.start()

    def quarter(number):
        count = 32 if number < 3 else 31
        pltpu.make_async_copy(grecv.at[pl.ds(0, count)], grecv.at[pl.ds(0, count)], g_recv.at[number]).wait()
        sources = [
            lax.rem(first_block + DEVICES // 8 - (4 * number + turn), DEVICES // 8) for turn in range(1, 5)
        ]
        for place, block in enumerate(sources):
            eight = grecv[pl.ds(pl.multiple_of(block * 8, 8), 8)].reshape(128, 128)
            arrived[:, place * 128 : (place + 1) * 128] = jnp.transpose(eight.astype(F32)).astype(BF)

        def select(step, carry):
            base = pl.multiple_of(step * 256, 256)
            marks = jnp.concatenate(
                [oneslot[pl.ds(pl.multiple_of(block * 128, 128), 128), pl.ds(base, 256)] for block in sources], axis=0
            )
            found = dot(arrived[...], marks)
            if number > 0:
                found = found + landed[:, pl.ds(base, 256)]
            if number < 3:
                landed[:, pl.ds(base, 256)] = found
            else:
                late = (slot[0:1, pl.ds(base, 256)] // 16) % 2 == 1
                forcing = jnp.where(late, found[CH : 2 * CH], found[0:CH])
                begun = ocean[:, pl.ds(base, 256)].astype(F32) + forcing
                window[:, pl.ds(base + HALO, 256)] = begun.astype(BF)
            return carry

        lax.fori_loop(0, OCN // 256, select, 0, unroll=4)

    for number in range(4):
        quarter(number)

    previous = where_of(lax.rem(me + DEVICES - 1, DEVICES))
    following = where_of(lax.rem(me + 1, DEVICES))

    def ocean_rims(buffer, first):
        return [
            pltpu.make_async_remote_copy(
                src_ref=buffer.at[:, HALO : 2 * HALO], dst_ref=buffer.at[:, EXT - HALO : EXT],
                send_sem=o_send.at[first], recv_sem=o_recv.at[first], device_id=previous, device_id_type=MESH,
            ),
            pltpu.make_async_remote_copy(
                src_ref=buffer.at[:, OCN : OCN + HALO], dst_ref=buffer.at[:, 0:HALO],
                send_sem=o_send.at[first + 1], recv_sem=o_recv.at[first + 1], device_id=following, device_id_type=MESH,
            ),
        ]

    def mix(buffer, number, block):
        base = pl.multiple_of(block * 256, 256)
        segments = jnp.concatenate(
            [buffer[:, pl.ds(pl.multiple_of(base + 256 * part, 256), 256)] for part in range(3)], axis=0
        )
        groups = []
        for tap in range(TAPS):
            index = taps_in[tap : tap + 1, pl.ds(base, 256)] - base
            part_of = index // 256
            found = dot(segments, onehot(iota((256, 256), 0) == index % 256))
            chosen = jnp.where(
                part_of == 0, found[0:CH], jnp.where(part_of == 1, found[CH : 2 * CH], found[2 * CH : 3 * CH])
            )
            groups.append(chosen.astype(BF))
        return dot(mweights[number], jnp.concatenate(groups, axis=0))

    def hidden_block(block):
        total = mix(window, 0, block)
        base = pl.multiple_of(block * 256, 256)
        hwindow[:, pl.ds(base + HALO, 256)] = jax.nn.gelu(total, approximate=True).astype(BF)

    def last_block(block):
        total = mix(hwindow, 1, block)
        base = pl.multiple_of(block * 256, 256)
        ocean_done[:, pl.ds(base, 256)] = (window[:, pl.ds(base + HALO, 256)].astype(F32) + total).astype(BF)

    def close_ends(buffer):
        @pl.when(me == 0)
        def _():
            buffer[:, 0:HALO] = jnp.zeros((CH, HALO), BF)

        @pl.when(me == DEVICES - 1)
        def _():
            buffer[:, EXT - HALO : EXT] = jnp.zeros((CH, HALO), BF)

    def layer(buffer, first, do_block, between):
        copies = ocean_rims(buffer, first)
        for copy in copies:
            copy.start()

        def middle(block, carry):
            do_block(block)
            return carry

        lax.fori_loop(1, 7, middle, 0, unroll=2)
        between()
        for copy in copies:
            copy.wait()
        close_ends(buffer)

        def ends(step, carry):
            do_block(step * 7)
            return carry

        lax.fori_loop(0, 2, ends, 0, unroll=2)

    stores = [
        pltpu.make_async_copy(ocean_done.at[:, first:last], ocean_out.at[:, first:last], local.at[number])
        for number, first, last in ((1, 256, 1792), (2, 0, 256), (3, 1792, 2048))
    ]
    layer(window, 0, hidden_block, lambda: None)
    layer(hwindow, 2, last_block, stores[0].start)
    stores[1].start()
    stores[2].start()
    for copy in stores:
        copy.wait()
    store.wait()

    pltpu.make_async_copy(vsend.at[pl.ds(0, DEVICES - 1)], vsend.at[pl.ds(0, DEVICES - 1)], a_send).wait()
    pltpu.make_async_copy(gsend.at[pl.ds(0, DEVICES - 1)], gsend.at[pl.ds(0, DEVICES - 1)], g_send).wait()


def hand_over(air, ocean, air_out, ocean_out, air_held, ocean_held, come, go):
    pieces = [(ocean, ocean_held, ocean_out)]
    for part in range(4):
        rows = pl.ds(part * 16, 16)
        pieces.append((air.at[rows], air_held.at[rows], air_out.at[rows]))
    inward = [pltpu.make_async_copy(src, held, come.at[i]) for i, (src, held, _) in enumerate(pieces)]
    outward = [pltpu.make_async_copy(held, dst, go.at[i]) for i, (_, held, dst) in enumerate(pieces)]
    for copy in inward:
        copy.start()
    for first, second in zip(inward, outward):
        first.wait()
        second.start()
    for copy in outward:
        copy.wait()


def shards(atmos, ocean, heat, w1, w2, m1, m2, slot, cells, taps):
    dma = pltpu.SemaphoreType.DMA
    anywhere = pl.BlockSpec(memory_space=pl.ANY)
    results = pl.pallas_call(
        kernel,
        out_shape=(
            jax.ShapeDtypeStruct((CH, AR, AC), BF),
            jax.ShapeDtypeStruct((CH, OCN), BF),
        ),
        in_specs=[anywhere] * 10,
        out_specs=(anywhere, anywhere),
        scratch_shapes=[
            pltpu.VMEM((CH, OCN), BF),
            pltpu.VMEM((1, CH), F32),
            pltpu.VMEM((1, OCN), I32),
            pltpu.VMEM((1, SLOTS), I32),
            pltpu.VMEM((CH, OCN), BF),
            pltpu.VMEM((CH, AR, AC), BF),
            pltpu.VMEM((3, 3, CH, CH), BF),
            pltpu.VMEM((3, 3, CH, CH), BF),
            pltpu.VMEM((TAPS, CH, CH), BF),
            pltpu.VMEM((TAPS, CH, CH), BF),
            pltpu.VMEM((TAPS, OCN), I32),
            pltpu.VMEM((CH, AR, AC), BF),
            pltpu.VMEM((AR, CH, AC), BF),
            pltpu.VMEM((DEVICES, 1, 256), F32),
            pltpu.VMEM((DEVICES, 1, 256), F32),
            pltpu.VMEM((2, CH, 128), BF),
            pltpu.VMEM((6, CH, 128), BF),
            pltpu.VMEM((40, 768), F32),
            pltpu.VMEM((AR + 4, CH, RING), BF),
            pltpu.VMEM((AR + 2, CH, RING), BF),
            pltpu.VMEM((2, CH, RING), F32),
            pltpu.VMEM((2, 3 * CH, 3 * CH), BF),
            pltpu.VMEM((2 * CAP, SLOTS), BF),
            pltpu.VMEM((AC, SLOTS), BF),
            pltpu.VMEM((DEVICES, 16, 128), BF),
            pltpu.VMEM((DEVICES, 16, 128), BF),
            pltpu.VMEM((128, 512), BF),
            pltpu.VMEM((128, OCN), F32),
            pltpu.VMEM((OCN, OCN), BF),
            pltpu.VMEM((2, CH, TAPS * CH), BF),
            pltpu.VMEM((CH, EXT), BF),
            pltpu.VMEM((CH, EXT), BF),
            dma((10,)), dma, dma, dma((8,)), dma((8,)), dma((8,)), dma((8,)), dma, dma((4,)), dma((4,)), dma((4,)),
        ],
        compiler_params=pltpu.CompilerParams(
            collective_id=0, has_side_effects=True, vmem_limit_bytes=56 << 20
        ),
        name="level",
    )(atmos, ocean, heat.reshape(1, CH), w1, w2, m1, m2, slot.reshape(1, OCN), cells, taps)
    return pl.pallas_call(
        hand_over,
        out_shape=(
            jax.ShapeDtypeStruct((CH, AR, AC), BF),
            jax.ShapeDtypeStruct((CH, OCN), BF),
        ),
        in_specs=[anywhere, anywhere],
        out_specs=(anywhere, anywhere),
        scratch_shapes=[pltpu.VMEM((CH, AR, AC), BF), pltpu.VMEM((CH, OCN), BF), dma((5,)), dma((5,))],
        name="hand_over",
    )(*results)


def solution(mesh):
    placed = (
        P(None, "tile", "face"),
        P(None, ("face", "tile")),
        P(),
        P(),
        P(),
        P(),
        P(),
        P(("face", "tile")),
        P(("face", "tile"), None),
        P(None, ("face", "tile")),
    )
    return jax.shard_map(
        shards,
        mesh=mesh,
        in_specs=placed,
        out_specs=(P(None, "tile", "face"), P(None, ("face", "tile"))),
        check_vma=False,
    )
```

```python
import jax
import jax.numpy as jnp
from jax import lax
from jax.experimental import pallas as pl
from jax.experimental.pallas import tpu as pltpu
from jax.sharding import PartitionSpec as P

MESH = pl.DeviceIdType.MESH
BF = jnp.bfloat16
F32 = jnp.float32
I32 = jnp.int32
FACES = 4
TILES = 32
DEVICES = 128
CAP = 32
CH = 64
AR = 24
AC = 512
OCN = 2048
SLOTS = 4096
HALO = 256
EXT = OCN + 2 * HALO
RING = AC + 128
TAPS = 9


def iota(shape, dim):
    return lax.broadcasted_iota(I32, shape, dim)


def dot(a, b):
    return jnp.dot(a, b, preferred_element_type=F32)


def dot_nt(a, b):
    return lax.dot_general(a, b, (((1,), (1,)), ((), ())), preferred_element_type=F32)


def onehot(mask):
    return jnp.where(mask, 1.0, 0.0).astype(BF)


def where_of(number):
    return (lax.div(number, TILES), lax.rem(number, TILES))


def kernel(
    air, ocean_hbm, heat_hbm, w1, w2, m1, m2, slot_hbm, cells_hbm, taps,
    air_out, ocean_out,
    ocean, heat, slot, cells, ocean_done,
    air_in, w1_in, w2_in, m1_in, m2_in, taps_in, air_done, after,
    vsend, vrecv, cols, rcols, sst, sx, hx, acc, weights, picked_cols, onecol,
    gsend, grecv, arrived, landed, oneslot, mweights, window, hwindow,
    local, a_send, a_recv, r_send, r_recv, s_send, s_recv, g_send, g_recv, o_send, o_recv,
):
    face = lax.axis_index("face")
    tile = lax.axis_index("tile")
    me = face * TILES + tile

    up = lax.rem(tile + TILES - 1, TILES)
    down = lax.rem(tile + 1, TILES)
    west = lax.rem(face + FACES - 1, FACES)
    east = lax.rem(face + 1, FACES)
    around = (
        (face, up), (face, down), (west, tile), (east, tile),
        (west, up), (west, down), (east, up), (east, down),
    )

    loads = [
        pltpu.make_async_copy(src, dst, local.at[number])
        for number, (src, dst) in enumerate(
            (
                (slot_hbm, slot), (ocean_hbm, ocean), (cells_hbm, cells), (heat_hbm, heat), (air, air_in),
                (w1, w1_in), (w2, w2_in), (m1, m1_in), (m2, m2_in), (taps, taps_in),
            )
        )
    ]
    for copy in loads:
        copy.start()

    barrier = pltpu.get_barrier_semaphore()

    def greet(step, carry):
        pl.semaphore_signal(
            barrier, inc=1, device_id=where_of(lax.rem(me + step, DEVICES)), device_id_type=MESH
        )
        return carry

    lax.fori_loop(0, 42, lambda step, carry: greet(3 * step + 3, greet(3 * step + 2, greet(3 * step + 1, carry))), 0)
    greet(127, 0)

    for copy in loads[:2]:
        copy.wait()

    slots = slot[...]
    heat_row = ocean[0:16, :].astype(F32)[0:1]
    here = iota((128, OCN), 0) == slots % CAP + CAP * lax.rem(me, 4)
    values = jnp.concatenate([jnp.where(here, heat_row, 0.0).astype(BF), onehot(here)], axis=0)
    source = onehot(iota((DEVICES, OCN), 0) == slots // CAP)
    vsend[:, 0, :] = dot_nt(source, values)
    pl.semaphore_wait(barrier, DEVICES - 1)

    def send_values(step, carry):
        other = lax.rem(me + step, DEVICES)
        pltpu.make_async_remote_copy(
            src_ref=vsend.at[other], dst_ref=vrecv.at[me], send_sem=a_send, recv_sem=a_recv,
            device_id=where_of(other), device_id_type=MESH,
        ).start()
        return carry

    lax.fori_loop(0, 42, lambda step, carry: send_values(3 * step + 3, send_values(3 * step + 2, send_values(3 * step + 1, carry))), 0)
    send_values(127, 0)
    vrecv[me] = vsend[me]

    for copy in loads[2:]:
        copy.wait()
    def rim(number, src, dst, send, recv):
        return pltpu.make_async_remote_copy(
            src_ref=src, dst_ref=dst, send_sem=send.at[number], recv_sem=recv.at[number],
            device_id=around[number], device_id_type=MESH,
        )

    for first in (0, 16):
        sx[first + 2 : first + 10, :, 0:AC] = pltpu.einshape("crw->rcw", air_in[:, first : first + 8, :])
    air_rims = [
        rim(0, sx.at[2:4, :, 0:AC], sx.at[AR + 2 : AR + 4, :, 0:AC], r_send, r_recv),
        rim(1, sx.at[AR : AR + 2, :, 0:AC], sx.at[0:2, :, 0:AC], r_send, r_recv),
    ]
    for copy in air_rims:
        copy.start()
    sx[10:18, :, 0:AC] = pltpu.einshape("crw->rcw", air_in[:, 8:16, :])

    lane = iota((CH, 128), 1)

    def pack_row(row, carry):
        left, right = carry
        first = jnp.where(lane < 2, sx[row + 2, :, 0:128].astype(F32), 0.0)
        last = jnp.where(lane >= 126, sx[row + 2, :, AC - 128 : AC].astype(F32), 0.0)
        left = left + pltpu.roll(first, 2 * row, 1)
        right = right + pltpu.roll(last, 2 * row + 2, 1)
        return left, right

    zero = jnp.zeros((CH, 128), F32)
    left, right = lax.fori_loop(0, AR, pack_row, (zero, zero), unroll=6)
    cols[0] = left.astype(BF)
    cols[1] = right.astype(BF)

    column_rims = [
        rim(2, cols.at[0], rcols.at[1], r_send, r_recv),
        rim(3, cols.at[1], rcols.at[0], r_send, r_recv),
        rim(4, cols.at[0], rcols.at[5], r_send, r_recv),
        rim(5, cols.at[0], rcols.at[3], r_send, r_recv),
        rim(6, cols.at[1], rcols.at[4], r_send, r_recv),
        rim(7, cols.at[1], rcols.at[2], r_send, r_recv),
    ]
    for copy in column_rims:
        copy.start()
    air_rims += column_rims

    def make_columns(step, carry):
        base = pl.multiple_of(step * 256, 256)
        column = cells[0:1, pl.ds(base, 256)] % AC
        onecol[:, pl.ds(base, 256)] = onehot(iota((AC, 256), 0) == column)
        return carry

    lax.fori_loop(0, SLOTS // 256, make_columns, 0, unroll=2)
    for number, weight in enumerate((w1_in, w2_in)):
        for row_tap in range(3):
            for col_tap in range(3):
                weights[number, row_tap * CH : (row_tap + 1) * CH, col_tap * CH : (col_tap + 1) * CH] = weight[
                    row_tap, col_tap
                ]
    for number, weight in enumerate((m1_in, m2_in)):
        for tap in range(TAPS):
            mweights[number, :, tap * CH : (tap + 1) * CH] = weight[tap]
    def make_slots(step, carry):
        base = pl.multiple_of(step * 256, 256)
        mark = slot[0:1, pl.ds(base, 256)]
        row = mark // CAP * 16 + mark % 16

        def fill(part, inner_carry):
            first = pl.multiple_of(part * 256, 256)
            oneslot[pl.ds(first, 256), pl.ds(base, 256)] = onehot(iota((256, 256), 0) + first == row)
            return inner_carry

        return lax.fori_loop(0, OCN // 256, fill, carry)

    lax.fori_loop(0, OCN // 256, make_slots, 0)

    channel_weight = jnp.sum(
        jnp.where(iota((CH, CH), 0) == iota((CH, CH), 1), heat[...], 0.0), axis=1, keepdims=True
    )

    pltpu.make_async_copy(vrecv.at[pl.ds(0, DEVICES - 1)], vrecv.at[pl.ds(0, DEVICES - 1)], a_recv).wait()
    for block in range(SLOTS // 128):
        base = block * 128
        line = (vrecv[4 * block] + vrecv[4 * block + 1]) + (vrecv[4 * block + 2] + vrecv[4 * block + 3])
        hit = iota((CAP, 128), 0) == cells[0:1, base : base + 128] // AC
        for kind in range(2):
            picked_cols[CAP * kind : CAP * (kind + 1), base : base + 128] = jnp.where(
                hit, line[:, kind * 128 : (kind + 1) * 128], 0.0
            ).astype(BF)
    sums = dot_nt(picked_cols[...], onecol[...])
    sst[8 : 8 + AR, 128 : 128 + AC] = sums[0:AR] / jnp.maximum(sums[CAP : CAP + AR], 1.0)

    top, low, far = 128, 640, 768
    sst_rims = [
        rim(0, sst.at[8:16, top:low], sst.at[32:40, top:low], s_send, s_recv),
        rim(1, sst.at[24:32, top:low], sst.at[0:8, top:low], s_send, s_recv),
        rim(2, sst.at[8:32, 128:256], sst.at[8:32, low:far], s_send, s_recv),
        rim(3, sst.at[8:32, 512:640], sst.at[8:32, 0:128], s_send, s_recv),
        rim(4, sst.at[8:16, 128:256], sst.at[32:40, low:far], s_send, s_recv),
        rim(5, sst.at[24:32, 128:256], sst.at[0:8, low:far], s_send, s_recv),
        rim(6, sst.at[8:16, 512:640], sst.at[32:40, 0:128], s_send, s_recv),
        rim(7, sst.at[24:32, 512:640], sst.at[0:8, 0:128], s_send, s_recv),
    ]
    for copy in sst_rims:
        copy.start()
    def begin(row, carry):
        line = sst[pl.ds(row + 8, 1), 128 : 128 + AC]
        state = sx[row + 2, :, 0:AC].astype(F32) + channel_weight * line
        sx[row + 2, :, 0:AC] = state.astype(BF)
        return carry

    for copy in air_rims:
        copy.wait()
    lax.fori_loop(0, AR, begin, 0, unroll=6)

    def ring_block(row, left, right):
        from_right = pltpu.roll(right, lax.rem(128 - 2 * row, 128), 1)
        from_left = pltpu.roll(left, lax.rem(254 - 2 * row, 128), 1)
        return jnp.where(lane < 64, from_right, from_left).astype(BF)

    def extend(row, carry):
        sx[row + 2, :, AC:RING] = ring_block(row, rcols[0].astype(F32), rcols[1].astype(F32))
        return carry

    lax.fori_loop(0, AR, extend, 0, unroll=6)
    for row in range(2):
        sx[row, :, AC:RING] = ring_block(jnp.int32(AR - 2 + row), rcols[2].astype(F32), rcols[3].astype(F32))
        sx[AR + 2 + row, :, AC:RING] = ring_block(jnp.int32(row), rcols[4].astype(F32), rcols[5].astype(F32))

    for copy in sst_rims:
        copy.wait()

    low_lane = iota((1, 128), 1) < 64

    def begin_block(row, inside):
        whole = sst[pl.ds(row + 6, 1), :]
        line = jnp.where(low_lane, whole[:, 640:768], whole[:, 0:128])
        state = sx[row, :, AC:RING].astype(F32) + channel_weight * line
        sx[row, :, AC:RING] = jnp.where(inside, state, 0.0).astype(BF)

    def begin_side(row, carry):
        begin_block(row + 2, True)
        return carry

    lax.fori_loop(0, AR, begin_side, 0, unroll=6)
    for row in (0, 1, AR + 2, AR + 3):
        inside = tile > 0 if row < 2 else tile < TILES - 1
        state = sx[row, :, 0:AC].astype(F32) + channel_weight * sst[row + 6 : row + 7, 128 : 128 + AC]
        sx[row, :, 0:AC] = jnp.where(inside, state, 0.0).astype(BF)
        begin_block(row, inside)

    def three(x, width):
        west_of = pltpu.roll(x, 1, 1)[:, 0:width]
        east_of = pltpu.roll(x, RING - 1, 1)[:, 0:width]
        return jnp.concatenate([west_of, x[:, 0:width], east_of], axis=0)

    def first_conv(row, carry):
        part = dot(weights[0], three(sx[row], RING))
        total = acc[0] + part[2 * CH : 3 * CH]
        acc[0] = acc[1] + part[CH : 2 * CH]
        acc[1] = part[0:CH]
        middle = row - 2
        inside = jnp.logical_and(jnp.logical_or(middle >= 1, tile > 0), jnp.logical_or(middle < AR + 1, tile < TILES - 1))
        hidden = jnp.where(inside, jax.nn.gelu(total, approximate=True), 0.0)
        hx[jnp.maximum(middle, 0)] = hidden.astype(BF)
        return carry

    lax.fori_loop(0, AR + 4, first_conv, 0, unroll=7)

    def second_conv(row, carry):
        part = dot(weights[1], three(hx[row], AC))
        total = acc[0, :, 0:AC] + part[2 * CH : 3 * CH]
        acc[0, :, 0:AC] = acc[1, :, 0:AC] + part[CH : 2 * CH]
        acc[1, :, 0:AC] = part[0:CH]
        middle = jnp.maximum(row - 2, 0)
        after[middle] = (sx[middle + 2, :, 0:AC].astype(F32) + total).astype(BF)
        return carry

    lax.fori_loop(0, AR + 2, second_conv, 0, unroll=13)

    first_block = lax.div(me, 8)

    def block_of(step):
        return lax.rem(first_block + step, DEVICES // 8)

    def find(block):
        base = pl.multiple_of(block * 256, 256)
        row = cells[0:1, pl.ds(base, 256)] // AC
        select = onecol[:, pl.ds(base, 256)]
        state = jnp.zeros((CH, 256), F32)
        for part in range(AR // 4):
            rows = after[part * 4 : part * 4 + 4].reshape(4 * CH, AC)
            found = dot(rows, select)
            for inner in range(4):
                state = jnp.where(row == part * 4 + inner, found[inner * CH : (inner + 1) * CH], state)
        return state

    def ship(state, block, others, number):
        flat = jnp.transpose(state).reshape(8, CAP, CH)
        pair = jnp.concatenate([flat[:, 0:16], flat[:, 16:32]], axis=2)
        gsend[pl.ds(pl.multiple_of(block * 8, 8), 8)] = pair.astype(BF)
        for inner in others:
            other = block * 8 + inner
            pltpu.make_async_remote_copy(
                src_ref=gsend.at[other], dst_ref=grecv.at[me], send_sem=g_send, recv_sem=g_recv.at[number],
                device_id=where_of(other), device_id_type=MESH,
            ).start()

    def coupling(step, state):
        found = find(block_of(step))
        ship(state, block_of(step - 1), range(8), lax.div(step - 2, 4))
        return found

    state = lax.fori_loop(2, DEVICES // 8 + 1, coupling, find(block_of(1)), unroll=5)
    ship(state, first_block, [lax.rem(me + step, 8) for step in range(1, 8)], 3)
    grecv[me] = gsend[me]

    air_done[...] = pltpu.einshape("rcw->crw", after[...])
    store = pltpu.make_async_copy(air_done, air_out, local.at[0])
    store.start()

    def quarter(number):
        count = 32 if number < 3 else 31
        pltpu.make_async_copy(grecv.at[pl.ds(0, count)], grecv.at[pl.ds(0, count)], g_recv.at[number]).wait()
        sources = [
            lax.rem(first_block + DEVICES // 8 - (4 * number + turn), DEVICES // 8) for turn in range(1, 5)
        ]
        for place, block in enumerate(sources):
            eight = grecv[pl.ds(pl.multiple_of(block * 8, 8), 8)].reshape(128, 128)
            arrived[:, place * 128 : (place + 1) * 128] = jnp.transpose(eight.astype(F32)).astype(BF)

        def select(step, carry):
            base = pl.multiple_of(step * 256, 256)
            marks = jnp.concatenate(
                [oneslot[pl.ds(pl.multiple_of(block * 128, 128), 128), pl.ds(base, 256)] for block in sources], axis=0
            )
            found = dot(arrived[...], marks)
            if number > 0:
                found = found + landed[:, pl.ds(base, 256)]
            if number < 3:
                landed[:, pl.ds(base, 256)] = found
            else:
                late = (slot[0:1, pl.ds(base, 256)] // 16) % 2 == 1
                forcing = jnp.where(late, found[CH : 2 * CH], found[0:CH])
                begun = ocean[:, pl.ds(base, 256)].astype(F32) + forcing
                window[:, pl.ds(base + HALO, 256)] = begun.astype(BF)
            return carry

        lax.fori_loop(0, OCN // 256, select, 0, unroll=4)

    for number in range(4):
        quarter(number)

    previous = where_of(lax.rem(me + DEVICES - 1, DEVICES))
    following = where_of(lax.rem(me + 1, DEVICES))

    def ocean_rims(buffer, first):
        return [
            pltpu.make_async_remote_copy(
                src_ref=buffer.at[:, HALO : 2 * HALO], dst_ref=buffer.at[:, EXT - HALO : EXT],
                send_sem=o_send.at[first], recv_sem=o_recv.at[first], device_id=previous, device_id_type=MESH,
            ),
            pltpu.make_async_remote_copy(
                src_ref=buffer.at[:, OCN : OCN + HALO], dst_ref=buffer.at[:, 0:HALO],
                send_sem=o_send.at[first + 1], recv_sem=o_recv.at[first + 1], device_id=following, device_id_type=MESH,
            ),
        ]

    def lane_pick(wide, index):
        halves = []
        for half in range(2):
            reach = jnp.broadcast_to(index[:, half * 128 : (half + 1) * 128] - 128 * half, (8, 128))
            inner = reach % 128
            part_of = reach // 128
            groups = []
            for group in range(CH // 8):
                parts = []
                for part in range(half, half + 5):
                    row = (part // 2) * CH + group * 8
                    column = (part % 2) * 128
                    parts.append(wide[row : row + 8, column : column + 128])
                found = jnp.take_along_axis(parts[0], inner, axis=1)
                for part in range(1, 5):
                    found = jnp.where(part_of == part, jnp.take_along_axis(parts[part], inner, axis=1), found)
                groups.append(found)
            halves.append(jnp.concatenate(groups, axis=0))
        return jnp.concatenate(halves, axis=1)

    def mix(buffer, number, block):
        base = pl.multiple_of(block * 256, 256)
        segments = jnp.concatenate(
            [buffer[:, pl.ds(pl.multiple_of(base + 256 * part, 256), 256)] for part in range(3)], axis=0
        )
        wide = segments.astype(F32)
        groups = []
        for tap in range(TAPS):
            index = taps_in[tap : tap + 1, pl.ds(base, 256)] - base
            if tap % 3 == 2:
                groups.append(lane_pick(wide, index).astype(BF))
                continue
            part_of = index // 256
            found = dot(segments, onehot(iota((256, 256), 0) == index % 256))
            chosen = jnp.where(
                part_of == 0, found[0:CH], jnp.where(part_of == 1, found[CH : 2 * CH], found[2 * CH : 3 * CH])
            )
            groups.append(chosen.astype(BF))
        return dot(mweights[number], jnp.concatenate(groups, axis=0))

    def hidden_block(block):
        total = mix(window, 0, block)
        base = pl.multiple_of(block * 256, 256)
        hwindow[:, pl.ds(base + HALO, 256)] = jax.nn.gelu(total, approximate=True).astype(BF)

    def last_block(block):
        total = mix(hwindow, 1, block)
        base = pl.multiple_of(block * 256, 256)
        ocean_done[:, pl.ds(base, 256)] = (window[:, pl.ds(base + HALO, 256)].astype(F32) + total).astype(BF)

    def close_ends(buffer):
        @pl.when(me == 0)
        def _():
            buffer[:, 0:HALO] = jnp.zeros((CH, HALO), BF)

        @pl.when(me == DEVICES - 1)
        def _():
            buffer[:, EXT - HALO : EXT] = jnp.zeros((CH, HALO), BF)

    def layer(buffer, first, do_block, between):
        copies = ocean_rims(buffer, first)
        for copy in copies:
            copy.start()

        def middle(block, carry):
            do_block(block)
            return carry

        lax.fori_loop(1, 7, middle, 0, unroll=2)
        between()
        for copy in copies:
            copy.wait()
        close_ends(buffer)

        def ends(step, carry):
            do_block(step * 7)
            return carry

        lax.fori_loop(0, 2, ends, 0, unroll=2)

    stores = [
        pltpu.make_async_copy(ocean_done.at[:, first:last], ocean_out.at[:, first:last], local.at[number])
        for number, first, last in ((1, 256, 1792), (2, 0, 256), (3, 1792, 2048))
    ]
    layer(window, 0, hidden_block, lambda: None)
    layer(hwindow, 2, last_block, stores[0].start)
    stores[1].start()
    stores[2].start()
    for copy in stores:
        copy.wait()
    store.wait()

    pltpu.make_async_copy(vsend.at[pl.ds(0, DEVICES - 1)], vsend.at[pl.ds(0, DEVICES - 1)], a_send).wait()
    pltpu.make_async_copy(gsend.at[pl.ds(0, DEVICES - 1)], gsend.at[pl.ds(0, DEVICES - 1)], g_send).wait()


def hand_over(air, ocean, air_out, ocean_out, air_held, ocean_held, come, go):
    pieces = [(ocean, ocean_held, ocean_out)]
    for part in range(4):
        rows = pl.ds(part * 16, 16)
        pieces.append((air.at[rows], air_held.at[rows], air_out.at[rows]))
    inward = [pltpu.make_async_copy(src, held, come.at[i]) for i, (src, held, _) in enumerate(pieces)]
    outward = [pltpu.make_async_copy(held, dst, go.at[i]) for i, (_, held, dst) in enumerate(pieces)]
    for copy in inward:
        copy.start()
    for first, second in zip(inward, outward):
        first.wait()
        second.start()
    for copy in outward:
        copy.wait()


def shards(atmos, ocean, heat, w1, w2, m1, m2, slot, cells, taps):
    dma = pltpu.SemaphoreType.DMA
    anywhere = pl.BlockSpec(memory_space=pl.ANY)
    results = pl.pallas_call(
        kernel,
        out_shape=(
            jax.ShapeDtypeStruct((CH, AR, AC), BF),
            jax.ShapeDtypeStruct((CH, OCN), BF),
        ),
        in_specs=[anywhere] * 10,
        out_specs=(anywhere, anywhere),
        scratch_shapes=[
            pltpu.VMEM((CH, OCN), BF),
            pltpu.VMEM((1, CH), F32),
            pltpu.VMEM((1, OCN), I32),
            pltpu.VMEM((1, SLOTS), I32),
            pltpu.VMEM((CH, OCN), BF),
            pltpu.VMEM((CH, AR, AC), BF),
            pltpu.VMEM((3, 3, CH, CH), BF),
            pltpu.VMEM((3, 3, CH, CH), BF),
            pltpu.VMEM((TAPS, CH, CH), BF),
            pltpu.VMEM((TAPS, CH, CH), BF),
            pltpu.VMEM((TAPS, OCN), I32),
            pltpu.VMEM((CH, AR, AC), BF),
            pltpu.VMEM((AR, CH, AC), BF),
            pltpu.VMEM((DEVICES, 1, 256), F32),
            pltpu.VMEM((DEVICES, 1, 256), F32),
            pltpu.VMEM((2, CH, 128), BF),
            pltpu.VMEM((6, CH, 128), BF),
            pltpu.VMEM((40, 768), F32),
            pltpu.VMEM((AR + 4, CH, RING), BF),
            pltpu.VMEM((AR + 2, CH, RING), BF),
            pltpu.VMEM((2, CH, RING), F32),
            pltpu.VMEM((2, 3 * CH, 3 * CH), BF),
            pltpu.VMEM((2 * CAP, SLOTS), BF),
            pltpu.VMEM((AC, SLOTS), BF),
            pltpu.VMEM((DEVICES, 16, 128), BF),
            pltpu.VMEM((DEVICES, 16, 128), BF),
            pltpu.VMEM((128, 512), BF),
            pltpu.VMEM((128, OCN), F32),
            pltpu.VMEM((OCN, OCN), BF),
            pltpu.VMEM((2, CH, TAPS * CH), BF),
            pltpu.VMEM((CH, EXT), BF),
            pltpu.VMEM((CH, EXT), BF),
            dma((10,)), dma, dma, dma((8,)), dma((8,)), dma((8,)), dma((8,)), dma, dma((4,)), dma((4,)), dma((4,)),
        ],
        compiler_params=pltpu.CompilerParams(
            collective_id=0, has_side_effects=True, vmem_limit_bytes=56 << 20
        ),
        name="level",
    )(atmos, ocean, heat.reshape(1, CH), w1, w2, m1, m2, slot.reshape(1, OCN), cells, taps)
    return pl.pallas_call(
        hand_over,
        out_shape=(
            jax.ShapeDtypeStruct((CH, AR, AC), BF),
            jax.ShapeDtypeStruct((CH, OCN), BF),
        ),
        in_specs=[anywhere, anywhere],
        out_specs=(anywhere, anywhere),
        scratch_shapes=[pltpu.VMEM((CH, AR, AC), BF), pltpu.VMEM((CH, OCN), BF), dma((5,)), dma((5,))],
        name="hand_over",
    )(*results)


def solution(mesh):
    placed = (
        P(None, "tile", "face"),
        P(None, ("face", "tile")),
        P(),
        P(),
        P(),
        P(),
        P(),
        P(("face", "tile")),
        P(("face", "tile"), None),
        P(None, ("face", "tile")),
    )
    return jax.shard_map(
        shards,
        mesh=mesh,
        in_specs=placed,
        out_specs=(P(None, "tile", "face"), P(None, ("face", "tile"))),
        check_vma=False,
    )
```
